256 devices in a mesh: dp: 8 (over z_hi, y), seq: 32 (over z_lo, x, core).
Axes of the slice: x: 4, y: 4, z: 8 (z_hi: 2, z_lo: 4; z = z_hi * 4 + z_lo), core: 2. Of those that a mesh axis runs over, the one named last changes fastest.
Arguments:
- q_img: bfloat16 [8, 4096, 2048], P('dp', 'seq'), may hold values from -6 to 6
- k_img: bfloat16 [8, 4096, 2048], P('dp', 'seq'), may hold values from -6 to 6
- v_img: bfloat16 [8, 4096, 2048], P('dp', 'seq'), may hold values from -12 to 12
- x_txt: bfloat16 [8, 77, 2432], P('dp'), may hold values from -9 to 9
- w_txt: bfloat16 [3, 2432, 2048], P(None, 'dp', 'seq'), may hold values from -0.125 to 0.125
- grad_img: bfloat16 [8, 4096, 2048], P('dp', 'seq'), may hold values from -6 to 6
- grad_txt: bfloat16 [8, 77, 2048], P('dp', None, 'seq'), may hold values from -6 to 6
Outputs:
- o_img: bfloat16 [8, 4096, 2048], P('dp', 'seq')
- o_txt: bfloat16 [8, 77, 2048], P('dp', None, 'seq')
- grad_qkv_img: bfloat16 [3, 8, 4096, 2048], P(None, 'dp', 'seq')
- dx_txt: float32 [8, 77, 2432], P('dp', None, 'seq')
- dw_txt: float32 [3, 2432, 2048], P(None, 'dp', 'seq')
The draws below stay inside these ranges and needn't reach their ends.
All inputs are finite; a program needn't handle non-finite values.
Results may differ from the reference program's by a relative error of at most 0.014.
Values may be sent and summed in bfloat16 or wider, within the bound.
No kernel may reach another device: no remote copies, remote signals or barrier semaphores. Data moves between devices by JAX's collectives and lax.ppermute only.
A program may use at most 64 MiB of HBM per device.

```python
import math
import jax
import jax.numpy as jnp
from jax import lax

D = 2432
HEADS = 32
HEAD_DIM = 64
TXT = 77
HD = 2048
IMG = 4096
SAMPLES = 8


def draw_q_img(key, part):
    base = jnp.clip(1.5 * jax.random.normal(jax.random.fold_in(key, 1), (SAMPLES, IMG, HD), jnp.float32), -6.0, 6.0)
    return base.astype(jnp.bfloat16)


def draw_k_img(key, part):
    base = jnp.clip(1.5 * jax.random.normal(jax.random.fold_in(key, 2), (SAMPLES, IMG, HD), jnp.float32), -6.0, 6.0)
    return base.astype(jnp.bfloat16)


def levels(stream_key, extent, split, smallest, largest):
    factor_of = 1.0
    for position, parts in split:
        heights = jax.random.uniform(jax.random.fold_in(jax.random.fold_in(stream_key, 6), position), (parts,), jnp.float32, smallest / len(split), largest / len(split))
        factor_of = factor_of * jnp.repeat(jnp.exp(heights), extent[position] // parts).reshape((-1,) + (1,) * (len(extent) - 1 - position))
    return factor_of


def gaussian(stream_key, dims, spread, reach, pieces=(), held_as=jnp.bfloat16):
    loudness = levels(stream_key, dims, pieces, -0.22, 0.18) if pieces else 1.0
    result = jax.random.normal(stream_key, dims, jnp.float32) * spread * loudness
    return jnp.minimum(jnp.maximum(result, -reach), reach).astype(held_as)


def setup_inputs(seed: int = 0) -> dict:
    streams_of = jax.random.split(jax.random.key(seed), 8)
    return {
        "q_img": draw_q_img(jax.random.fold_in(streams_of[7], 71), 0),
        "k_img": draw_k_img(jax.random.fold_in(streams_of[7], 71), 0),
        "v_img": gaussian(streams_of[2], (SAMPLES, IMG, HD), 2.0, 12.0, ((0, 8), (1, 32))),
        "x_txt": gaussian(streams_of[3], (SAMPLES, TXT, D), 1.5, 9.0, ((0, 8),)),
        "w_txt": gaussian(streams_of[4], (3, D, HD), D ** -0.5, 0.125, ((1, 8), (2, 32))),
        "grad_img": gaussian(streams_of[5], (SAMPLES, IMG, HD), 1.0, 6.0, ((0, 8), (1, 32))),
        "grad_txt": gaussian(streams_of[6], (SAMPLES, TXT, HD), 1.0, 6.0, ((0, 8), (2, 32))),
    }


def attend(query, keys, values, cotangent):
    scale = 1.0 / math.sqrt(HEAD_DIM)
    scores = jnp.dot(query, keys.T, preferred_element_type=jnp.float32) * scale
    shifted = jnp.exp(scores - lax.optimization_barrier(jnp.max(scores, axis=1, keepdims=True)))
    probs = shifted / lax.optimization_barrier(jnp.sum(shifted, axis=1, keepdims=True))
    probs_b = probs.astype(jnp.bfloat16)
    joint_o = jnp.dot(probs_b, values, preferred_element_type=jnp.float32).astype(jnp.bfloat16)
    value_grads = jnp.dot(probs_b.T, cotangent, preferred_element_type=jnp.float32).astype(jnp.bfloat16)
    prob_grads = jnp.dot(cotangent, values.T, preferred_element_type=jnp.float32)
    row_terms = lax.optimization_barrier(jnp.sum(cotangent.astype(jnp.float32) * joint_o.astype(jnp.float32), axis=1, keepdims=True))
    score_grads = (probs * (prob_grads - row_terms)).astype(jnp.bfloat16)
    query_grads = (jnp.dot(score_grads, keys, preferred_element_type=jnp.float32) * scale).astype(jnp.bfloat16)
    key_grads = (jnp.dot(score_grads.T, query, preferred_element_type=jnp.float32) * scale).astype(jnp.bfloat16)
    return (joint_o, query_grads, key_grads, value_grads)

def reference(q_img, k_img, v_img, x_txt, w_txt, grad_img, grad_txt):
    text_qkv = jnp.einsum('std,idh->isth', x_txt.astype(jnp.float32), w_txt.astype(jnp.float32)).astype(jnp.bfloat16)
    length = IMG + TXT

    def to_heads(image_part, text_part):
        whole = jnp.concatenate([image_part, text_part], axis=1)
        whole = whole.reshape(SAMPLES, length, HEADS, HEAD_DIM).transpose(0, 2, 1, 3)
        return whole.reshape(SAMPLES * HEADS, length, HEAD_DIM)

    def from_heads(stacked):
        whole = stacked.reshape(SAMPLES, HEADS, length, HEAD_DIM).transpose(0, 2, 1, 3).reshape(SAMPLES, length, HD)
        return (whole[:, :IMG], whole[:, IMG:])
    inputs = (to_heads(q_img, text_qkv[0]), to_heads(k_img, text_qkv[1]), to_heads(v_img, text_qkv[2]), to_heads(grad_img, grad_txt))
    joint_o, query_grads, key_grads, value_grads = lax.map(lambda items: attend(*items), inputs)
    o_img, o_txt = from_heads(joint_o)
    dq_image, dq_text = from_heads(query_grads)
    dk_image, dk_text = from_heads(key_grads)
    dv_image, dv_text = from_heads(value_grads)
    grad_qkv_img = jnp.stack([dq_image, dk_image, dv_image])
    text_grads = jnp.stack([dq_text, dk_text, dv_text])
    dw_txt = jnp.einsum('std,isth->idh', x_txt.astype(jnp.float32), text_grads.astype(jnp.float32))
    dx_txt = jnp.einsum('isth,idh->std', text_grads.astype(jnp.float32), w_txt.astype(jnp.float32))
    return (o_img, o_txt, grad_qkv_img, dx_txt, dw_txt)
```

```python
import functools

import jax
import jax.numpy as jnp
from jax import lax
from jax.experimental import pallas as pl
from jax.experimental.pallas import tpu as pltpu
from jax.sharding import PartitionSpec as P

bf16, f32 = jnp.bfloat16, jnp.float32
SDS = jax.ShapeDtypeStruct
LOG2E = 1.4426950408889634
DEVS = 32
TOK = 128
HALF = TOK // 2
IMG = DEVS * TOK
TXT = 77
TXT_PAD = 128
TXT_HALF = TXT_PAD // 2
KEYS = IMG + TXT_PAD
STEPS = 4
SRC_STEP = DEVS // STEPS
IMG_STEP = SRC_STEP * HALF
TXT_STEP = TXT_HALF // STEPS
ROWS = IMG_STEP + TXT_STEP
DX_ROWS = 48
EX_ROWS = IMG // 2 + TXT_HALF + TXT_PAD
CHUNK = 1024
VMEM = 60 << 20


def dot(a, b, ca, cb):
    return lax.dot_general(a, b, (((ca,), (cb,)), ((), ())), preferred_element_type=f32)


def low_lanes():
    return lax.broadcasted_iota(jnp.int32, (1, 128), 1) < 64


def swap(x):
    return jnp.concatenate([x[..., 64:], x[..., :64]], axis=-1)


def params(**kw):
    return pltpu.CompilerParams(vmem_limit_bytes=VMEM, **kw)


def whole(shape):
    return pl.BlockSpec(shape, lambda *i: (0,) * len(shape))


def cost(us):
    return pl.CostEstimate(flops=int(us * 1.15e9), bytes_accessed=1 << 20, transcendentals=0)


def pack_kernel(q_ref, k_ref, v_ref, g_ref, w_ref, x0_ref, x1_ref, w_out):
    low = low_lanes()
    tiles = q_ref.shape[1] // 128
    for c in range(tiles):
        cols = slice(128 * c, 128 * c + 128)
        q = q_ref[:, cols] * jnp.asarray(0.125, bf16)
        k, v, g = k_ref[:, cols], v_ref[:, cols], g_ref[:, cols]
        for which, (a, b) in enumerate(((q, g), (k, v))):
            first = jnp.where(low, a, swap(b))
            second = jnp.where(low, swap(a), b)
            for core in range(2):
                rows = slice(HALF * core, HALF * core + HALF)
                x0_ref[2 * c + core, which] = first[rows]
                x1_ref[2 * c + core, which] = second[rows]

    @pl.when(pl.program_id(0) == 0)
    def _():
        n = w_ref.shape[1]
        w_out[0:n] = jnp.concatenate([w_ref[0], w_ref[1]], axis=1)
        w_out[n : n + n // 2] = jnp.concatenate([w_ref[2, : n // 2], w_ref[2, n // 2 :]], axis=1)


def pack(q, k, v, g, w):
    n = w.shape[1]
    grid = 4
    cols = q.shape[1] // grid
    part = pl.BlockSpec((TOK, cols), lambda i: (0, i))
    out = pl.BlockSpec((DEVS // grid, 2, HALF, 128), lambda i: (i, 0, 0, 0))
    return pl.pallas_call(
        pack_kernel,
        grid=(grid,),
        out_shape=(
            SDS((DEVS, 2, HALF, 128), bf16),
            SDS((DEVS, 2, HALF, 128), bf16),
            SDS((n + n // 2, 128), bf16),
        ),
        in_specs=[part] * 4 + [whole(w.shape)],
        out_specs=(out, out, whole((n + n // 2, 128))),
        name="pack",
        cost_estimate=cost(4),
        compiler_params=params(),
    )(q, k, v, g, w)


def project_kernel(order_ref, x_ref, w_ref, g_ref, out_ref):
    qk = jnp.zeros((TXT, 128), f32)
    va = jnp.zeros((TXT, 128), f32)
    vb = jnp.zeros((TXT, 128), f32)
    blocks, n = w_ref.shape[0], x_ref.shape[2]
    for r in range(blocks):
        x = x_ref[order_ref[r]]
        qk += dot(x, w_ref[r, 0:n], 1, 0)
        va += dot(x[:, : n // 2], w_ref[r, n:], 1, 0)
        vb += dot(x[:, n // 2 :], w_ref[r, n:], 1, 0)
    v = va[:, :64] + vb[:, 64:]
    q = qk[:, :64].astype(bf16) * jnp.asarray(0.125, bf16)
    k = qk[:, 64:].astype(bf16)
    out_ref[...] = jnp.zeros_like(out_ref)
    out_ref[0:TXT] = jnp.concatenate([q, g_ref[...]], axis=1)
    out_ref[TXT_PAD : TXT_PAD + TXT] = jnp.concatenate([k, v.astype(bf16)], axis=1)


def project(order, x8, w, g):
    return pl.pallas_call(
        project_kernel,
        out_shape=SDS((2 * TXT_PAD, 128), bf16),
        in_specs=[pl.BlockSpec(memory_space=pltpu.SMEM)] + [pl.BlockSpec(memory_space=pltpu.VMEM)] * 3,
        out_specs=pl.BlockSpec(memory_space=pltpu.VMEM),
        name="project",
        cost_estimate=cost(3),
        compiler_params=params(),
    )(order, x8, w, g)


def key_chunks():
    return [(j, min(CHUNK, IMG - j)) for j in range(0, IMG, CHUNK)] + [(IMG, TXT_PAD)]


def attend_kernel(
    q_ref, tq_ref, k0_ref, k1_ref, tk_ref, out_ref, own_ref, ex_ref, dt_ref,
    kv, kz, vz, kvt, s_ref, e_ref, ds_ref, acc,
):
    step = pl.program_id(0)
    low = low_lanes()

    @pl.when(step == 0)
    def _():
        for j, n, src in ((0, IMG // 2, k0_ref), (IMG // 2, IMG // 2, k1_ref), (IMG, TXT_PAD, tk_ref)):
            x = src[...].reshape(n, 128)
            kz[j : j + n] = jnp.where(low, x, jnp.zeros_like(x))
            vz[j : j + n] = jnp.where(low, jnp.zeros_like(x), x)
            kvt[:, j : j + n] = x.T
        acc[...] = jnp.zeros_like(acc)

    qg = jnp.concatenate([q_ref[...].reshape(IMG_STEP, 128), tq_ref[...]], axis=0)
    padding = lax.broadcasted_iota(jnp.int32, (1, TXT_PAD), 1) >= TXT
    top = jnp.full((ROWS, 128), -jnp.inf, f32)
    for j, n in key_chunks():
        s = dot(qg, kz[j : j + n], 1, 1)
        if j == IMG:
            s = jnp.where(padding, -1e30, s)
        s_ref[:, j : j + n] = s
        for i in range(0, n, 128):
            top = jnp.maximum(top, s[:, i : i + 128])
    top = jnp.max(top, axis=1, keepdims=True) * LOG2E
    total = jnp.zeros((ROWS, 128), f32)
    for j, n in key_chunks():
        e = jnp.exp2(s_ref[:, j : j + n] * LOG2E - top)
        for i in range(0, n, 128):
            total = total + e[:, i : i + 128]
        e_ref[:, j : j + n] = e.astype(bf16)
    o = dot(kvt[...], e_ref[...], 1, 1).T
    inv = 1.0 / jnp.sum(total, axis=1, keepdims=True)
    o = (o * inv).astype(bf16).astype(f32)
    qf = qg.astype(f32)
    row_term = jnp.sum(jnp.where(low, 0.0, qf * o), axis=1, keepdims=True) * inv
    qs = jnp.where(low, qf, qf * inv).astype(bf16)
    qst = qs.T
    for j, n in key_chunks():
        dp = dot(qs, vz[j : j + n], 1, 1)
        e = e_ref[:, j : j + n]
        ds = (e.astype(f32) * (dp - row_term)).astype(bf16)
        ds_ref[:, j : j + n] = ds
        acc[0:64, j : j + n] += dot(qst[0:64], ds, 1, 0)
        acc[64:128, j : j + n] += dot(qst[64:128], e, 1, 0)
    dq = dot(kvt[...], ds_ref[...], 1, 1).T
    r = jnp.where(low, dq * 0.125, o).astype(bf16)
    out_ref[...] = r[:IMG_STEP].reshape(out_ref.shape)
    at = pl.multiple_of(IMG // 2 + TXT_STEP * step, 16)
    ex_ref[pl.ds(at, TXT_STEP)] = r[IMG_STEP:]

    @pl.when(step == STEPS - 1)
    def _():
        own_ref[...] = acc[:, : IMG // 2].T.reshape(own_ref.shape).astype(bf16)
        ex_ref[: IMG // 2] = acc[:, IMG // 2 : IMG].T.astype(bf16)
        dt = acc[:, IMG:].T
        dt_ref[...] = dt
        ex_ref[IMG // 2 + TXT_HALF :] = dt.astype(bf16)


def attend(received, tq, other, tk, name):
    half = (DEVS, HALF, 128)
    return pl.pallas_call(
        attend_kernel,
        grid=(STEPS,),
        out_shape=(SDS(half, bf16), SDS(half, bf16), SDS((EX_ROWS, 128), bf16), SDS((TXT_PAD, 128), f32)),
        in_specs=[
            pl.BlockSpec((SRC_STEP, None, HALF, 128), lambda i: (i, 0, 0, 0)),
            pl.BlockSpec((TXT_STEP, 128), lambda i: (i, 0)),
            pl.BlockSpec((DEVS, None, HALF, 128), lambda i: (0, 1, 0, 0)),
            whole(half),
            whole((TXT_PAD, 128)),
        ],
        out_specs=(
            pl.BlockSpec((SRC_STEP, HALF, 128), lambda i: (i, 0, 0)),
            whole(half),
            whole((EX_ROWS, 128)),
            whole((TXT_PAD, 128)),
        ),
        scratch_shapes=[
            pltpu.VMEM((8, 128), bf16),
            pltpu.VMEM((KEYS, 128), bf16),
            pltpu.VMEM((KEYS, 128), bf16),
            pltpu.VMEM((128, KEYS), bf16),
            pltpu.VMEM((ROWS, KEYS), f32),
            pltpu.VMEM((ROWS, KEYS), bf16),
            pltpu.VMEM((ROWS, KEYS), bf16),
            pltpu.VMEM((128, KEYS), f32),
        ],
        name=name,
        cost_estimate=cost(43),
        compiler_params=params(),
    )(received, tq, received, other, tk)


def finish_kernel(dqo_ref, own_ref, got_ref, y_ref):
    y_ref[:, :HALF] = dqo_ref[...]
    for i in range(DEVS):
        got = got_ref[HALF * i : HALF * i + HALF].astype(f32)
        y_ref[i, HALF:] = (own_ref[i].astype(f32) + got).astype(bf16)


def finish(dqo, own, got):
    return pl.pallas_call(
        finish_kernel,
        out_shape=SDS((DEVS, TOK, 128), bf16),
        in_specs=[pl.BlockSpec(memory_space=pltpu.VMEM)] * 3,
        out_specs=pl.BlockSpec(memory_space=pltpu.VMEM),
        name="finish_first",
        cost_estimate=cost(3),
        compiler_params=params(),
    )(dqo, own, got)


def text_rows(core, ex_ref, got_ref, dt_ref, scratch):
    tail = slice(IMG // 2, IMG // 2 + TXT_HALF)
    scratch[pl.ds(pl.multiple_of(TXT_HALF * core, 64), TXT_HALF)] = ex_ref[tail]
    scratch[pl.ds(pl.multiple_of(TXT_HALF * (1 - core), 64), TXT_HALF)] = got_ref[tail]
    sums = dt_ref[...] + got_ref[IMG // 2 + TXT_HALF :].astype(f32)
    return scratch[...], sums.astype(bf16)


def finish_last_kernel(
    ids_ref, dqo_ref, own_ref, ex0_ref, got0_ref, dt0_ref, ex1_ref, got1_ref, dt1_ref, w_ref, w_other_ref,
    y_ref, tg_ref, o_ref, rows_ref, g_own, g_other,
):
    core = ids_ref[0]
    low = low_lanes()
    y_ref[:, :HALF] = dqo_ref[...]
    for i in range(DEVS):
        got = got1_ref[HALF * i : HALF * i + HALF].astype(f32)
        y_ref[i, HALF:TOK] = (own_ref[i].astype(f32) + got).astype(bf16)
    qo0, kv0 = text_rows(core, ex0_ref, got0_ref, dt0_ref, rows_ref)
    qo1, kv1 = text_rows(core, ex1_ref, got1_ref, dt1_ref, rows_ref)
    first = core == 0
    for mine, target in ((first, g_own), (jnp.logical_not(first), g_other)):
        qo, kv = jnp.where(mine, qo0, qo1), jnp.where(mine, kv0, kv1)
        target[0] = jnp.where(low, qo, swap(kv))
        target[1] = jnp.where(low, swap(kv), jnp.zeros_like(kv))
        target[2] = jnp.where(low, jnp.zeros_like(kv), kv)
    o_ref[...] = jnp.where(first, qo0, qo1)[:TXT, 64:]
    tg_ref[0:80] = g_own[0, 0:80]
    tg_ref[80:160] = g_own[1, 0:80]
    here = pl.ds(pl.multiple_of(DX_ROWS * core, 16), DX_ROWS)
    n = w_ref.shape[1] * 2 // 3
    for r in range(w_ref.shape[0]):
        terms = []
        for grads, weights in ((g_own, w_ref), (g_other, w_other_ref)):
            qk = dot(grads[0, here], weights[r, 0:n], 1, 1)
            va = dot(grads[1, here], weights[r, n:], 1, 1)
            vb = dot(grads[2, here], weights[r, n:], 1, 1)
            terms.append(qk + jnp.concatenate([va, vb], axis=1))
        block = (terms[0] + terms[1]).astype(bf16)
        n4 = n // 4
        for part in range(4):
            piece = block[:, n4 * part : n4 * part + n4]
            piece = jnp.concatenate([piece, jnp.zeros((DX_ROWS, 128 - n4), bf16)], axis=1)
            y_ref[4 * ids_ref[1 + r] + part, TOK:] = piece


def finish_last(ids, dqo, own, ex0, got0, dt0, ex1, got1, dt1, w, w_other):
    v = pl.BlockSpec(memory_space=pltpu.VMEM)
    return pl.pallas_call(
        finish_last_kernel,
        out_shape=(SDS((DEVS, TOK + DX_ROWS, 128), bf16), SDS((160, 128), bf16), SDS((TXT, 64), bf16)),
        in_specs=[pl.BlockSpec(memory_space=pltpu.SMEM)] + [v] * 10,
        out_specs=(v, v, v),
        scratch_shapes=[
            pltpu.VMEM((TXT_PAD, 128), bf16),
            pltpu.VMEM((3, TXT_PAD, 128), bf16),
            pltpu.VMEM((3, TXT_PAD, 128), bf16),
        ],
        name="finish_last",
        cost_estimate=cost(5),
        compiler_params=params(),
    )(ids, dqo, own, ex0, got0, dt0, ex1, got1, dt1, w, w_other)


def unpack_kernel(z0_ref, z1_ref, o_ref, g_ref, dx_ref, acc):
    low = low_lanes()
    step = pl.program_id(0)
    for c in range(z0_ref.shape[0] // 2):
        cols = slice(128 * c, 128 * c + 128)
        for core in range(2):
            rows = slice(HALF * core, HALF * core + HALF)
            a, b = z0_ref[2 * c + core], z1_ref[2 * c + core]
            qo0, qo1, kv0, kv1 = a[:HALF], b[:HALF], a[HALF:TOK], b[HALF:TOK]
            g_ref[0, rows, cols] = jnp.where(low, qo0, swap(qo1))
            o_ref[rows, cols] = jnp.where(low, swap(qo0), qo1)
            g_ref[1, rows, cols] = jnp.where(low, kv0, swap(kv1))
            g_ref[2, rows, cols] = jnp.where(low, swap(kv0), kv1)
    for core in range(2):
        total = z1_ref[core, TOK:].astype(f32)
        for c in range(1, z0_ref.shape[0] // 2):
            total = total + z1_ref[2 * c + core, TOK:].astype(f32)
        rows = slice(DX_ROWS * core, DX_ROWS * core + DX_ROWS)

        @pl.when(step == 0)
        def _():
            acc[rows] = total

        @pl.when(step > 0)
        def _():
            acc[rows] += total

    dx_ref[...] = acc[: dx_ref.shape[0], : dx_ref.shape[1]]


def unpack(z0, z1, dx_cols):
    grid = 4
    cols = 2048 // grid
    return pl.pallas_call(
        unpack_kernel,
        grid=(grid,),
        out_shape=(SDS((TOK, 2048), bf16), SDS((3, TOK, 2048), bf16), SDS((TXT, dx_cols), f32)),
        in_specs=[
            pl.BlockSpec((DEVS // grid, TOK, 128), lambda i: (i, 0, 0)),
            pl.BlockSpec((DEVS // grid, TOK + DX_ROWS, 128), lambda i: (i, 0, 0)),
        ],
        out_specs=(
            pl.BlockSpec((TOK, cols), lambda i: (0, i)),
            pl.BlockSpec((3, TOK, cols), lambda i: (0, 0, i)),
            whole((TXT, dx_cols)),
        ),
        scratch_shapes=[pltpu.VMEM((2 * DX_ROWS, 128), f32)],
        name="unpack",
        cost_estimate=cost(4),
        compiler_params=params(),
    )(z0, z1)


def weight_grad_kernel(x_ref, tg_ref, out_ref):
    n = x_ref.shape[2]
    qk = jnp.zeros((n, 128), f32)
    v = jnp.zeros((n, 128), f32)
    for r in range(x_ref.shape[0]):
        qk += dot(x_ref[r], tg_ref[r, 0:TXT], 0, 0)
        v += dot(x_ref[r], tg_ref[r, 80 : 80 + TXT], 0, 0)
    out_ref[0] = qk[:, :64]
    out_ref[1] = qk[:, 64:]
    out_ref[2] = v[:, :64]


def weight_grad(x, tg):
    v = pl.BlockSpec(memory_space=pltpu.VMEM)
    return pl.pallas_call(
        weight_grad_kernel,
        out_shape=SDS((3, x.shape[2], 64), f32),
        in_specs=[v, v],
        out_specs=v,
        name="weight_grad",
        cost_estimate=cost(4),
        compiler_params=params(),
    )(x, tg)


def local(q_img, k_img, v_img, x_txt, w_txt, grad_img, grad_txt):
    seq, dp = lax.axis_index("seq"), lax.axis_index("dp")
    core = seq % 2
    dp_hi, dp_lo = dp // 4, dp % 4
    pair = [(i, i ^ 1) for i in range(DEVS)]
    across = [(i, i ^ 4) for i in range(8)]
    turns = [[(i, i // 4 * 4 + (i + k) % 4) for i in range(8)] for k in range(1, 4)]

    def gather_dp(x):
        both = jnp.stack([x, lax.ppermute(x, "dp", across)])
        return jnp.concatenate([both] + [lax.ppermute(both, "dp", t) for t in turns])

    order = jnp.stack(
        [(dp_hi ^ side) * 4 + (dp_lo + 4 - k) % 4 for k in range(4) for side in range(2)]
    ).astype(jnp.int32)

    x0, x1, w_own = pack(q_img[0], k_img[0], v_img[0], grad_img[0], w_txt)
    r0 = lax.all_to_all(x0, "seq", 0, 0, tiled=True)
    weights = gather_dp(w_own)
    x8 = x_txt[0].reshape(TXT, 8, -1).transpose(1, 0, 2)
    text = project(order, x8, weights, grad_txt[0])
    text_other = lax.ppermute(text, "seq", pair)
    weights_other = lax.ppermute(weights, "seq", pair)
    text0 = jnp.where(core == 0, text, text_other)
    text1 = jnp.where(core == 0, text_other, text)

    def phase(received, text_of_head, name):
        other = lax.ppermute(received[:, 1], "seq", pair)
        tq = lax.dynamic_slice_in_dim(text_of_head, TXT_HALF * core, TXT_HALF, 0)
        dqo, own, ex, dt = attend(received, tq, other, text_of_head[TXT_PAD:], name)
        return dqo, own, ex, dt, lax.ppermute(ex, "seq", pair)

    r1 = lax.all_to_all(x1, "seq", 0, 0, tiled=True)
    dqo0, own0, ex0, dt0, got0 = phase(r0, text0, "attend_first")
    z0 = lax.all_to_all(finish(dqo0, own0, got0), "seq", 0, 0, tiled=True)
    dqo1, own1, ex1, dt1, got1 = phase(r1, text1, "attend_second")

    xs = x8.reshape(2, 4, TXT, -1)
    kept = lax.dynamic_index_in_dim(xs, dp_hi, 0, keepdims=False)
    sent = lax.dynamic_index_in_dim(xs, 1 - dp_hi, 0, keepdims=False)
    both = jnp.stack([kept, lax.ppermute(sent, "dp", across)], axis=1)
    columns = [lax.dynamic_index_in_dim(both, (dp_lo + k) % 4, 0, keepdims=False) for k in range(4)]
    x_all = jnp.concatenate([columns[0]] + [lax.ppermute(c, "dp", t) for c, t in zip(columns[1:], turns)])

    ids = jnp.concatenate([core[None].astype(jnp.int32), order])
    y1, text_grads, o_txt = finish_last(
        ids, dqo1, own1, ex0, got0, dt0, ex1, got1, dt1, weights, weights_other
    )
    z1 = lax.all_to_all(y1, "seq", 0, 0, tiled=True)
    dw = weight_grad(x_all, gather_dp(text_grads))
    o_img, grads, dx = unpack(z0, z1, x_txt.shape[2] // DEVS)
    return o_img[None], o_txt[None], grads[:, None], dx[None], dw


def solution(mesh):
    in_specs = (
        P("dp", "seq", None),
        P("dp", "seq", None),
        P("dp", "seq", None),
        P("dp", None, None),
        P(None, "dp", "seq"),
        P("dp", "seq", None),
        P("dp", None, "seq"),
    )
    out_specs = (
        P("dp", "seq", None),
        P("dp", None, "seq"),
        P(None, "dp", "seq", None),
        P("dp", None, "seq"),
        P(None, "dp", "seq"),
    )
    return jax.shard_map(local, mesh=mesh, in_specs=in_specs, out_specs=out_specs, check_vma=False)
```

```python
import functools

import jax
import jax.numpy as jnp
from jax import lax
from jax.experimental import pallas as pl
from jax.experimental.pallas import tpu as pltpu
from jax.sharding import PartitionSpec as P

bf16, f32 = jnp.bfloat16, jnp.float32
SDS = jax.ShapeDtypeStruct
LOG2E = 1.4426950408889634
CHIPS = 16
TOK = 128
MINE = CHIPS * TOK
IMG = 2 * MINE
TXT = 77
TXT_ROWS = 80
TXT_PAD = 128
TXT_HALF = TXT_PAD // 2
KEYS = IMG + TXT_PAD
STEPS = 4
SRC_STEP = CHIPS // STEPS
ROWS = SRC_STEP * TOK
TAIL = TXT_HALF + TXT_PAD
CHUNK = 1024
VMEM = 40 << 20
IN_VMEM = pl.BlockSpec(memory_space=pltpu.VMEM)
IN_SMEM = pl.BlockSpec(memory_space=pltpu.SMEM)


def dot(a, b, ca, cb):
    return lax.dot_general(a, b, (((ca,), (cb,)), ((), ())), preferred_element_type=f32)


def low_lanes():
    return lax.broadcasted_iota(jnp.int32, (1, 128), 1) < 64


def swap(x):
    return jnp.concatenate([x[..., 64:], x[..., :64]], axis=-1)


def params():
    return pltpu.CompilerParams(vmem_limit_bytes=VMEM)


def whole(shape):
    return pl.BlockSpec(shape, lambda *i: (0,) * len(shape))


def cost(us):
    return pl.CostEstimate(flops=int(us * 1.15e9), bytes_accessed=1 << 20, transcendentals=0)


def pack_kernel(phase, q_ref, k_ref, v_ref, g_ref, x_ref):
    low = low_lanes()
    for c in range(q_ref.shape[1] // 128):
        cols = slice(128 * c, 128 * c + 128)
        q = q_ref[:, cols] * jnp.asarray(0.125, bf16)
        k, v, g = k_ref[:, cols], v_ref[:, cols], g_ref[:, cols]
        for which, (a, b) in enumerate(((q, g), (k, v))):
            if phase == 0:
                x_ref[c, which] = jnp.where(low, a, swap(b))
            else:
                x_ref[c, which] = jnp.where(low, swap(a), b)


def pack(phase, q, k, v, g, grid):
    part = pl.BlockSpec((TOK, q.shape[1] // grid), lambda i: (0, i))
    return pl.pallas_call(
        functools.partial(pack_kernel, phase),
        grid=(grid,),
        out_shape=SDS((CHIPS, 2, TOK, 128), bf16),
        in_specs=[part] * 4,
        out_specs=pl.BlockSpec((CHIPS // grid, 2, TOK, 128), lambda i: (i, 0, 0, 0)),
        name=("pack_first", "pack_second")[phase],
        cost_estimate=cost(3),
        compiler_params=params(),
    )(q, k, v, g)


def project_kernel(ids_ref, x_ref, w_ref, g_ref, out_ref):
    total = jnp.zeros((TXT, w_ref.shape[1]), f32)
    for r in range(w_ref.shape[0]):
        total += dot(x_ref[ids_ref[1 + r]], w_ref[r], 1, 1)
    total = total.astype(bf16)
    q = total[:, :64] * jnp.asarray(0.125, bf16)
    out_ref[...] = jnp.zeros_like(out_ref)
    out_ref[0:TXT] = jnp.concatenate([q, g_ref[...]], axis=1)
    out_ref[TXT_PAD : TXT_PAD + TXT] = total[:, 64:]


def project(ids, x8, w, g):
    return pl.pallas_call(
        project_kernel,
        out_shape=SDS((2 * TXT_PAD, 128), bf16),
        in_specs=[IN_SMEM] + [IN_VMEM] * 3,
        out_specs=IN_VMEM,
        name="project",
        cost_estimate=cost(3),
        compiler_params=params(),
    )(ids, x8, w, g)


def key_chunks():
    return [(j, min(CHUNK, IMG - j)) for j in range(0, IMG, CHUNK)] + [(IMG, TXT_PAD)]


def attend_kernel(
    phase, ids_ref, q_ref, own_kv_ref, other_kv_ref, text_ref, text_other_ref, y_ref, ex_ref, dt_ref,
    keys, values, kvt, s_ref, e_ref, acc,
):
    step = pl.program_id(0)
    core = ids_ref[0]
    mine = core == phase

    @pl.when(step == 0)
    def _():
        text = jnp.where(mine, text_ref[TXT_PAD:], text_other_ref[TXT_PAD:])
        for j, n, x in ((0, MINE, own_kv_ref), (MINE, MINE, other_kv_ref), (IMG, TXT_PAD, None)):
            t = (text if x is None else x[...].reshape(n, 128)).T
            cols = slice(j, j + n)
            kvt[0:128, cols] = t
            keys[0:64, cols] = t[:64]
            keys[64:128, cols] = t[:64]
            minus = lax.broadcasted_iota(jnp.int32, (64, n), 0) < 2
            values[0:64, cols] = jnp.where(minus, -1.0, 0.0).astype(bf16)
            values[64:128, cols] = t[64:]
        kvt[128:144] = jnp.ones((16, KEYS), bf16)
        acc[...] = jnp.zeros_like(acc)

    padding = lax.broadcasted_iota(jnp.int32, (1, TXT_PAD), 1) >= TXT

    def block(qg):
        rows = qg.shape[0]
        qgt = qg.T
        q = qg[:, :64].astype(f32) * LOG2E
        q_high = q.astype(bf16)
        left = jnp.concatenate([q_high, (q - q_high.astype(f32)).astype(bf16)], axis=1)
        top = jnp.full((rows, 128), -jnp.inf, f32)
        for j, n in key_chunks():
            s = dot(left, keys[:, j : j + n], 1, 0)
            if j == IMG:
                s = jnp.where(padding, -jnp.inf, s)
            s_ref[:rows, j : j + n] = s
            for i in range(0, n, 128):
                top = jnp.maximum(top, s[:, i : i + 128])
        top = jnp.max(top, axis=1, keepdims=True)
        ot = jnp.zeros((80, rows), f32)
        for j, n in key_chunks():
            e = jnp.exp2(s_ref[:rows, j : j + n] - top).astype(bf16)
            e_ref[:rows, j : j + n] = e
            ot = ot + dot(kvt[64:144, j : j + n], e, 1, 1)
        inv = 1.0 / ot[64:65]
        ot = (ot[:64] * inv).astype(bf16).astype(f32)
        gt = qgt[64:].astype(f32)
        row_term = jnp.sum(gt * ot, axis=0, keepdims=True) * inv
        gt = (gt * inv).astype(bf16)
        high = row_term.astype(bf16).astype(f32)
        left = jnp.concatenate([high, row_term - high, jnp.zeros((62, rows), f32), gt.astype(f32)], axis=0)
        left = left.astype(bf16).T
        dqt = jnp.zeros((64, rows), f32)
        for j, n in key_chunks():
            e = e_ref[:rows, j : j + n]
            ds = e * dot(left, values[:, j : j + n], 1, 0).astype(bf16)
            dqt = dqt + dot(kvt[0:64, j : j + n], ds, 1, 1)
            acc[0:64, j : j + n] += dot(qgt[0:64], ds, 1, 0)
            acc[64:128, j : j + n] += dot(gt, e, 1, 0)
        return jnp.concatenate([dqt * 0.125, ot], axis=0).T.astype(bf16)

    y_ref[pl.ds(SRC_STEP * step, SRC_STEP), :TOK] = block(q_ref[...].reshape(ROWS, 128)).reshape(SRC_STEP, TOK, 128)

    @pl.when(step == STEPS - 1)
    def _():
        rows = pl.ds(pl.multiple_of(TXT_HALF * core, TXT_HALF), TXT_HALF)
        ex_ref[:TXT_HALF] = block(jnp.where(mine, text_ref[rows], text_other_ref[rows]))
        dt = acc[:, IMG:].T
        dt_ref[...] = dt
        ex_ref[TXT_HALF:TAIL] = dt.astype(bf16)
        ex_ref[TAIL:] = acc[:, MINE:IMG].T.astype(bf16)
        y_ref[:, TOK : 2 * TOK] = acc[:, :MINE].T.astype(bf16).reshape(CHIPS, TOK, 128)


def attend(phase, ids, received, other, text, text_other, y_rows):
    half = (CHIPS, TOK, 128)
    text_shape = (2 * TXT_PAD, 128)
    return pl.pallas_call(
        functools.partial(attend_kernel, phase),
        grid=(STEPS,),
        out_shape=(
            SDS((CHIPS, y_rows, 128), bf16),
            SDS((TAIL + MINE, 128), bf16),
            SDS((TXT_PAD, 128), f32),
        ),
        in_specs=[
            IN_SMEM,
            pl.BlockSpec((SRC_STEP, None, TOK, 128), lambda i: (i, 0, 0, 0)),
            pl.BlockSpec((CHIPS, None, TOK, 128), lambda i: (0, 1, 0, 0)),
            whole(half),
            whole(text_shape),
            whole(text_shape),
        ],
        out_specs=(whole((CHIPS, y_rows, 128)), whole((TAIL + MINE, 128)), whole((TXT_PAD, 128))),
        scratch_shapes=[
            pltpu.VMEM((128, KEYS), bf16),
            pltpu.VMEM((128, KEYS), bf16),
            pltpu.VMEM((144, KEYS), bf16),
            pltpu.VMEM((ROWS, KEYS), f32),
            pltpu.VMEM((ROWS, KEYS), bf16),
            pltpu.VMEM((128, KEYS), f32),
        ],
        name=("attend_first", "attend_second")[phase],
        cost_estimate=cost(34),
        compiler_params=params(),
    )(ids, received, received, other, text, text_other)


def add_shares(y_in, got_ref, y_ref):
    for i in range(CHIPS):
        got = got_ref[TAIL + TOK * i : TAIL + TOK * i + TOK].astype(f32)
        y_ref[i] = (y_in[i].astype(f32) + got).astype(bf16)


def finish_first(y, got):
    part = pl.BlockSpec((CHIPS, TOK, 128), lambda i: (0, 1, 0))
    return pl.pallas_call(
        add_shares,
        grid=(1,),
        out_shape=SDS(y.shape, bf16),
        in_specs=[part, whole(got.shape)],
        out_specs=part,
        input_output_aliases={0: 0},
        name="finish_first",
        cost_estimate=cost(2),
        compiler_params=params(),
    )(y, got)


def text_kernel(ids_ref, ex0_ref, got0_ref, dt0_ref, ex1_ref, got1_ref, dt1_ref, own_ref, other_ref, o_ref, rows_ref):
    core = ids_ref[0]
    low = low_lanes()
    heads = []
    for ex, got, dt in ((ex0_ref, got0_ref, dt0_ref), (ex1_ref, got1_ref, dt1_ref)):
        rows_ref[pl.ds(pl.multiple_of(TXT_HALF * core, TXT_HALF), TXT_HALF)] = ex[:TXT_HALF]
        rows_ref[pl.ds(pl.multiple_of(TXT_HALF * (1 - core), TXT_HALF), TXT_HALF)] = got[:TXT_HALF]
        qo = rows_ref[0:TXT_ROWS]
        kv = (dt[...] + got[TXT_HALF:TAIL].astype(f32)).astype(bf16)[:TXT_ROWS]
        heads.append((qo, kv))
    for target, which in ((own_ref, core == 0), (other_ref, core == 1)):
        qo, kv = (jnp.where(which, a, b) for a, b in zip(*heads))
        vk = swap(kv)
        target[:, :128] = jnp.where(low, qo, vk)
        target[:, 128:] = jnp.where(low, vk, jnp.zeros_like(vk))
        if target is own_ref:
            o_ref[...] = qo[:TXT, 64:]


def text_grads(ids, shares):
    tail = whole((TAIL, 128))
    return pl.pallas_call(
        text_kernel,
        grid=(1,),
        out_shape=(SDS((TXT_ROWS, 256), bf16), SDS((TXT_ROWS, 256), bf16), SDS((TXT, 64), bf16)),
        in_specs=[IN_SMEM] + [tail, tail, whole((TXT_PAD, 128))] * 2,
        out_specs=(whole((TXT_ROWS, 256)), whole((TXT_ROWS, 256)), whole((TXT, 64))),
        scratch_shapes=[pltpu.VMEM((TXT_PAD, 128), bf16)],
        name="text_grads",
        cost_estimate=cost(2),
        compiler_params=params(),
    )(ids, *shares)


def finish_last_kernel(ids_ref, y_in, got_ref, own_ref, other_ref, w_ref, w_other_ref, y_ref):
    y_ref[:, :TOK] = y_in[:, :TOK]
    add_shares(y_in.at[:, TOK : 2 * TOK], got_ref, y_ref.at[:, TOK : 2 * TOK])
    first = ids_ref[0] == 0
    n = w_ref.shape[2] // 4
    for r in range(w_ref.shape[0]):
        total = dot(own_ref[:, :192], w_ref[r], 1, 0) + dot(other_ref[:, :192], w_other_ref[r], 1, 0)
        for i in range(2):
            at = 2 * n * i
            piece = jnp.where(first, total[:, at : at + n], total[:, at + n : at + 2 * n])
            piece = jnp.concatenate([piece, jnp.zeros((TXT_ROWS, 128 - n), f32)], axis=1)
            y_ref[2 * ids_ref[1 + r] + i, 2 * TOK :] = piece.astype(bf16)


def finish_last(ids, y, got, own, other, w, w_other):
    return pl.pallas_call(
        finish_last_kernel,
        out_shape=SDS(y.shape, bf16),
        in_specs=[IN_SMEM] + [IN_VMEM] * 6,
        out_specs=IN_VMEM,
        name="finish_last",
        cost_estimate=cost(5),
        compiler_params=params(),
    )(ids, y, got, own, other, w, w_other)


def unpack_kernel(z0_ref, z1_ref, o_ref, g_ref, dx_ref, acc):
    low = low_lanes()
    step = pl.program_id(0)
    total = jnp.zeros((TXT_ROWS, 128), f32)
    for c in range(z0_ref.shape[0]):
        cols = slice(128 * c, 128 * c + 128)
        qo0, qo1 = z0_ref[c, :TOK], z1_ref[c, :TOK]
        kv0, kv1 = z0_ref[c, TOK : 2 * TOK], z1_ref[c, TOK : 2 * TOK]
        g_ref[0, :, cols] = jnp.where(low, qo0, swap(qo1))
        o_ref[:, cols] = jnp.where(low, swap(qo0), qo1)
        g_ref[1, :, cols] = jnp.where(low, kv0, swap(kv1))
        g_ref[2, :, cols] = jnp.where(low, swap(kv0), kv1)
        total += z1_ref[c, 2 * TOK :].astype(f32)

    @pl.when(step == 0)
    def _():
        acc[...] = total

    @pl.when(step > 0)
    def _():
        acc[...] += total

    @pl.when(step == pl.num_programs(0) - 1)
    def _():
        dx_ref[...] = acc[...].T[: dx_ref.shape[0], :TXT].reshape(dx_ref.shape)


def unpack(z0, z1, dx_cols):
    grid = 4
    width = 128 * CHIPS
    return pl.pallas_call(
        unpack_kernel,
        grid=(grid,),
        out_shape=(SDS((TOK, width), bf16), SDS((3, TOK, width), bf16), SDS((dx_cols, 1, TXT), f32)),
        in_specs=[pl.BlockSpec((CHIPS // grid, z.shape[1], 128), lambda i: (i, 0, 0)) for z in (z0, z1)],
        out_specs=(
            pl.BlockSpec((TOK, width // grid), lambda i: (0, i)),
            pl.BlockSpec((3, TOK, width // grid), lambda i: (0, 0, i)),
            whole((dx_cols, 1, TXT)),
        ),
        scratch_shapes=[pltpu.VMEM((TXT_ROWS, 128), f32)],
        name="unpack",
        cost_estimate=cost(4),
        compiler_params=params(),
    )(z0, z1)


def weight_grad_kernel(x_ref, tg_ref, out_ref):
    total = jnp.zeros(out_ref.shape, f32)
    for r in range(x_ref.shape[0]):
        total += dot(tg_ref[r, :TXT, :192], x_ref[r], 0, 0)
    out_ref[...] = total


def weight_grad(x, tg):
    return pl.pallas_call(
        weight_grad_kernel,
        out_shape=SDS((192, x.shape[2]), f32),
        in_specs=[IN_VMEM] * 2,
        out_specs=IN_VMEM,
        name="weight_grad",
        cost_estimate=cost(4),
        compiler_params=params(),
    )(x, tg)


def local(q_img, k_img, v_img, x_txt, w_txt, grad_img, grad_txt):
    seq, dp = lax.axis_index("seq"), lax.axis_index("dp")
    core = seq % 2
    dp_hi, dp_lo = dp // 4, dp % 4
    pair = [(i, i ^ 1) for i in range(2 * CHIPS)]
    parity = [list(range(j, 2 * CHIPS, 2)) for j in range(2)]
    across = [(i, i ^ 4) for i in range(8)]
    turns = [[(i, i // 4 * 4 + (i + k) % 4) for i in range(8)] for k in range(1, 4)]

    def exchange(x):
        return lax.all_to_all(x, "seq", 0, 0, axis_index_groups=parity, tiled=True)

    def around(x, got):
        both = jnp.stack([x, got])
        return jnp.concatenate([both] + [lax.ppermute(both, "dp", t) for t in turns])

    order = [(dp_hi ^ side) * 4 + (dp_lo + 4 - k) % 4 for k in range(4) for side in range(2)]
    ids = jnp.stack([core] + order).astype(jnp.int32)
    image = (q_img[0], k_img[0], v_img[0], grad_img[0])

    w_own = jnp.swapaxes(w_txt, 1, 2).reshape(192, -1)
    w_across = lax.ppermute(w_own, "dp", across)

    x8 = x_txt[0].reshape(TXT, 8, -1).transpose(1, 0, 2)
    halves = x8.reshape(4, 2, TXT, -1)
    half = lax.dynamic_index_in_dim(halves, 2 * (1 - dp_hi) + core, 0, keepdims=False)
    packed = pack(0, *image, 4)
    packed, w_across = lax.optimization_barrier((packed, w_across))
    r0 = exchange(packed)
    weights = around(w_own, w_across)
    text = project(ids, x8, weights, grad_txt[0])
    text_other = lax.ppermute(text, "seq", pair)
    weights_other = lax.ppermute(weights, "seq", pair)
    second = pack(1, *image, 4)
    r0, second, text_other, weights_other, half = lax.optimization_barrier(
        (r0, second, text_other, weights_other, half)
    )

    kv0 = lax.ppermute(r0[:, 1], "seq", pair)
    r1 = exchange(second)
    x_half = lax.ppermute(half, "dp", across)
    y0, ex0, dt0 = attend(0, ids, r0, kv0, text, text_other, 2 * TOK)
    ex0, x_half = lax.optimization_barrier((ex0, x_half))
    got0 = lax.ppermute(ex0, "seq", pair)
    kv1 = lax.ppermute(r1[:, 1], "seq", pair)
    z0 = exchange(finish_first(y0, got0))
    y1, ex1, dt1 = attend(1, ids, r1, kv1, text, text_other, 2 * TOK + TXT_ROWS)
    got1 = lax.ppermute(ex1, "seq", pair)

    grads_own, grads_other, o_txt = text_grads(ids, (ex0, got0, dt0, ex1, got1, dt1))
    grads_across = lax.ppermute(grads_own, "dp", across)
    y1 = finish_last(ids, y1, got1, grads_own, grads_other, weights, weights_other)
    y1, grads_across, x_half = lax.optimization_barrier((y1, grads_across, x_half))
    z1 = exchange(y1)
    x_other = lax.ppermute(x_half, "seq", pair)
    x_across = jnp.where(core == 0, jnp.concatenate([x_half, x_other]), jnp.concatenate([x_other, x_half]))
    kept = lax.dynamic_slice_in_dim(x8, 4 * dp_hi, 4, 0)
    both = jnp.stack([kept, x_across], axis=1)
    columns = [lax.dynamic_index_in_dim(both, (dp_lo + k) % 4, 0, keepdims=False) for k in range(4)]
    x_all = jnp.concatenate([columns[0]] + [lax.ppermute(c, "dp", t) for c, t in zip(columns[1:], turns)])
    dw = weight_grad(x_all, around(grads_own, grads_across))
    dw = jnp.swapaxes(dw.reshape(3, 64, -1), 1, 2)
    o_img, grads, dx = unpack(z0, z1, x_txt.shape[2] // (2 * CHIPS))
    return o_img[None], o_txt[None], grads[:, None], dx.transpose(1, 2, 0), dw


def solution(mesh):
    in_specs = (
        P("dp", "seq", None),
        P("dp", "seq", None),
        P("dp", "seq", None),
        P("dp", None, None),
        P(None, "dp", "seq"),
        P("dp", "seq", None),
        P("dp", None, "seq"),
    )
    out_specs = (
        P("dp", "seq", None),
        P("dp", None, "seq"),
        P(None, "dp", "seq", None),
        P("dp", None, "seq"),
        P(None, "dp", "seq"),
    )
    return jax.shard_map(local, mesh=mesh, in_specs=in_specs, out_specs=out_specs, check_vma=False)
```

```python
import functools

import jax
import jax.numpy as jnp
from jax import lax
from jax.experimental import pallas as pl
from jax.experimental.pallas import tpu as pltpu
from jax.sharding import PartitionSpec as P

bf16, f32 = jnp.bfloat16, jnp.float32
SDS = jax.ShapeDtypeStruct
LOG2E = 1.4426950408889634
CHIPS = 16
TOK = 128
MINE = CHIPS * TOK
IMG = 2 * MINE
TXT = 77
TXT_ROWS = 80
TXT_PAD = 128
DX_ROWS = 48
TXT_HALF = TXT_PAD // 2
KEYS = IMG + TXT_PAD
STEPS = 4
SRC_STEP = CHIPS // STEPS
ROWS = SRC_STEP * TOK
TAIL = TXT_HALF + TXT_PAD
CHUNK = 1024
VMEM = 40 << 20
IN_VMEM = pl.BlockSpec(memory_space=pltpu.VMEM)
IN_SMEM = pl.BlockSpec(memory_space=pltpu.SMEM)


def dot(a, b, ca, cb):
    return lax.dot_general(a, b, (((ca,), (cb,)), ((), ())), preferred_element_type=f32)


def low_lanes():
    return lax.broadcasted_iota(jnp.int32, (1, 128), 1) < 64


def swap(x):
    return jnp.concatenate([x[..., 64:], x[..., :64]], axis=-1)


def params(limit=VMEM):
    return pltpu.CompilerParams(vmem_limit_bytes=limit)


def whole(shape):
    return pl.BlockSpec(shape, lambda *i: (0,) * len(shape))


def cost(us):
    return pl.CostEstimate(flops=int(us * 1.15e9), bytes_accessed=1 << 20, transcendentals=0)


def pack_kernel(phase, q_ref, k_ref, v_ref, g_ref, x_ref):
    low = low_lanes()
    for c in range(q_ref.shape[1] // 128):
        cols = slice(128 * c, 128 * c + 128)
        q = q_ref[:, cols] * jnp.asarray(0.125, bf16)
        k, v, g = k_ref[:, cols], v_ref[:, cols], g_ref[:, cols]
        for which, (a, b) in enumerate(((q, g), (k, v))):
            if phase == 0:
                x_ref[c, which] = jnp.where(low, a, swap(b))
            else:
                x_ref[c, which] = jnp.where(low, swap(a), b)


def pack(phase, q, k, v, g, grid):
    part = pl.BlockSpec((TOK, q.shape[1] // grid), lambda i: (0, i))
    return pl.pallas_call(
        functools.partial(pack_kernel, phase),
        grid=(grid,),
        out_shape=SDS((CHIPS, 2, TOK, 128), bf16),
        in_specs=[part] * 4,
        out_specs=pl.BlockSpec((CHIPS // grid, 2, TOK, 128), lambda i: (i, 0, 0, 0)),
        name=("pack_first", "pack_second")[phase],
        cost_estimate=cost(3),
        compiler_params=params(60 << 20),
    )(q, k, v, g)


def project_kernel(ids_ref, x_ref, w_ref, g_ref, out_ref, x8_ref, half_ref):
    total = jnp.zeros((TXT, w_ref.shape[1]), f32)
    n = w_ref.shape[2]
    for d in range(w_ref.shape[0]):
        x = x_ref[:, n * d : n * d + n]
        x8_ref[d] = x
        total += dot(x, w_ref[ids_ref[9 + d]], 1, 1)
    for i in range(half_ref.shape[0]):
        half_ref[i] = x8_ref[ids_ref[17] + i]
    total = total.astype(bf16)
    q = total[:, :64] * jnp.asarray(0.125, bf16)
    out_ref[...] = jnp.zeros_like(out_ref)
    out_ref[0:TXT] = jnp.concatenate([q, g_ref[...]], axis=1)
    out_ref[TXT_PAD : TXT_PAD + TXT] = total[:, 64:]


def project(ids, x, w, g):
    return pl.pallas_call(
        project_kernel,
        out_shape=(
            SDS((2 * TXT_PAD, 128), bf16),
            SDS((w.shape[0], TXT, w.shape[2]), bf16),
            SDS((2, TXT, w.shape[2]), bf16),
        ),
        in_specs=[IN_SMEM] + [IN_VMEM] * 3,
        out_specs=(IN_VMEM,) * 3,
        name="project",
        cost_estimate=cost(3),
        compiler_params=params(),
    )(ids, x, w, g)


def key_chunks():
    return [(j, min(CHUNK, IMG - j)) for j in range(0, IMG, CHUNK)] + [(IMG, TXT_PAD)]


def attend_kernel(
    phase, ids_ref, q_ref, own_kv_ref, other_kv_ref, text_ref, text_other_ref, y_ref, ex_ref, dt_ref,
    keys, values, kvt, s_ref, e_ref, acc,
):
    step = pl.program_id(0)
    core = ids_ref[0]
    mine = core == phase

    @pl.when(step == 0)
    def _():
        text = jnp.where(mine, text_ref[TXT_PAD:], text_other_ref[TXT_PAD:])
        for j, n, x in ((0, MINE, own_kv_ref), (MINE, MINE, other_kv_ref), (IMG, TXT_PAD, None)):
            t = (text if x is None else x[...].reshape(n, 128)).T
            cols = slice(j, j + n)
            kvt[0:128, cols] = t
            keys[0:64, cols] = t[:64]
            keys[64:128, cols] = t[:64]
            minus = lax.broadcasted_iota(jnp.int32, (64, n), 0) < 2
            values[0:64, cols] = jnp.where(minus, -1.0, 0.0).astype(bf16)
            values[64:128, cols] = t[64:]
        kvt[128:144] = jnp.ones((16, KEYS), bf16)
        acc[...] = jnp.zeros_like(acc)

    padding = lax.broadcasted_iota(jnp.int32, (1, TXT_PAD), 1) >= TXT

    def block(qg):
        rows = qg.shape[0]
        qgt = qg.T
        q = qg[:, :64].astype(f32) * LOG2E
        q_high = q.astype(bf16)
        left = jnp.concatenate([q_high, (q - q_high.astype(f32)).astype(bf16)], axis=1)
        top = jnp.full((rows, 128), -jnp.inf, f32)
        for j, n in key_chunks():
            s = dot(left, keys[:, j : j + n], 1, 0)
            if j == IMG:
                s = jnp.where(padding, -jnp.inf, s)
            s_ref[:rows, j : j + n] = s
            for i in range(0, n, 128):
                top = jnp.maximum(top, s[:, i : i + 128])
        top = jnp.max(top, axis=1, keepdims=True)
        ot = jnp.zeros((80, rows), f32)
        for j, n in key_chunks():
            e = jnp.exp2(s_ref[:rows, j : j + n] - top).astype(bf16)
            e_ref[:rows, j : j + n] = e
            ot = ot + dot(kvt[64:144, j : j + n], e, 1, 1)
        inv = 1.0 / ot[64:65]
        ot = (ot[:64] * inv).astype(bf16).astype(f32)
        gt = qgt[64:].astype(f32)
        row_term = jnp.sum(gt * ot, axis=0, keepdims=True) * inv
        gt = (gt * inv).astype(bf16)
        high = row_term.astype(bf16).astype(f32)
        left = jnp.concatenate([high, row_term - high, jnp.zeros((62, rows), f32), gt.astype(f32)], axis=0)
        left = left.astype(bf16).T
        dqt = jnp.zeros((64, rows), f32)
        chunks = key_chunks()

        def prob_grads(k):
            return dot(left, values[:, chunks[k][0] : chunks[k][0] + chunks[k][1]], 1, 0)

        dp = prob_grads(0)
        for k, (j, n) in enumerate(chunks):
            e = e_ref[:rows, j : j + n]
            ds = e * dp.astype(bf16)
            if k + 1 < len(chunks):
                dp = prob_grads(k + 1)
            dqt = dqt + dot(kvt[0:64, j : j + n], ds, 1, 1)
            acc[0:64, j : j + n] += dot(qgt[0:64], ds, 1, 0)
            acc[64:128, j : j + n] += dot(gt, e, 1, 0)
        return jnp.concatenate([dqt * 0.125, ot], axis=0).T.astype(bf16)

    y_ref[pl.ds(SRC_STEP * step, SRC_STEP), :TOK] = block(q_ref[...].reshape(ROWS, 128)).reshape(SRC_STEP, TOK, 128)

    @pl.when(step == STEPS - 1)
    def _():
        rows = pl.ds(pl.multiple_of(TXT_HALF * core, TXT_HALF), TXT_HALF)
        ex_ref[:TXT_HALF] = block(jnp.where(mine, text_ref[rows], text_other_ref[rows]))
        dt = acc[:, IMG:].T
        dt_ref[...] = dt
        ex_ref[TXT_HALF:TAIL] = dt.astype(bf16)
        ex_ref[TAIL:] = acc[:, MINE:IMG].T.astype(bf16)
        y_ref[:, TOK : 2 * TOK] = acc[:, :MINE].T.astype(bf16).reshape(CHIPS, TOK, 128)


def attend(phase, ids, received, other, text, text_other, y_rows):
    half = (CHIPS, TOK, 128)
    text_shape = (2 * TXT_PAD, 128)
    return pl.pallas_call(
        functools.partial(attend_kernel, phase),
        grid=(STEPS,),
        out_shape=(
            SDS((CHIPS, y_rows, 128), bf16),
            SDS((TAIL + MINE, 128), bf16),
            SDS((TXT_PAD, 128), f32),
        ),
        in_specs=[
            IN_SMEM,
            pl.BlockSpec((SRC_STEP, None, TOK, 128), lambda i: (i, 0, 0, 0)),
            pl.BlockSpec((CHIPS, None, TOK, 128), lambda i: (0, 1, 0, 0)),
            whole(half),
            whole(text_shape),
            whole(text_shape),
        ],
        out_specs=(whole((CHIPS, y_rows, 128)), whole((TAIL + MINE, 128)), whole((TXT_PAD, 128))),
        scratch_shapes=[
            pltpu.VMEM((128, KEYS), bf16),
            pltpu.VMEM((128, KEYS), bf16),
            pltpu.VMEM((144, KEYS), bf16),
            pltpu.VMEM((ROWS, KEYS), f32),
            pltpu.VMEM((ROWS, KEYS), bf16),
            pltpu.VMEM((128, KEYS), f32),
        ],
        name=("attend_first", "attend_second")[phase],
        cost_estimate=cost(34),
        compiler_params=params(),
    )(ids, received, received, other, text, text_other)


def add_shares(y_in, got_ref, y_ref):
    for i in range(CHIPS):
        got = got_ref[TAIL + TOK * i : TAIL + TOK * i + TOK].astype(f32)
        y_ref[i] = (y_in[i].astype(f32) + got).astype(bf16)


def finish_first(y, got):
    part = pl.BlockSpec((CHIPS, TOK, 128), lambda i: (0, 1, 0))
    return pl.pallas_call(
        add_shares,
        grid=(1,),
        out_shape=SDS(y.shape, bf16),
        in_specs=[part, whole(got.shape)],
        out_specs=part,
        input_output_aliases={0: 0},
        name="finish_first",
        cost_estimate=cost(2),
        compiler_params=params(),
    )(y, got)


def text_kernel(ids_ref, ex0_ref, got0_ref, dt0_ref, ex1_ref, got1_ref, dt1_ref, own_ref, other_ref, o_ref, rows_ref):
    core = ids_ref[0]
    low = low_lanes()
    heads = []
    for ex, got, dt in ((ex0_ref, got0_ref, dt0_ref), (ex1_ref, got1_ref, dt1_ref)):
        rows_ref[pl.ds(pl.multiple_of(TXT_HALF * core, TXT_HALF), TXT_HALF)] = ex[:TXT_HALF]
        rows_ref[pl.ds(pl.multiple_of(TXT_HALF * (1 - core), TXT_HALF), TXT_HALF)] = got[:TXT_HALF]
        qo = rows_ref[0:TXT_ROWS]
        kv = (dt[...] + got[TXT_HALF:TAIL].astype(f32)).astype(bf16)[:TXT_ROWS]
        heads.append((qo, kv))
    for target, which in ((own_ref, core == 0), (other_ref, core == 1)):
        qo, kv = (jnp.where(which, a, b) for a, b in zip(*heads))
        vk = swap(kv)
        target[:, :128] = jnp.where(low, qo, vk)
        target[:, 128:] = jnp.where(low, vk, jnp.zeros_like(vk))
        if target is own_ref:
            o_ref[...] = qo[:TXT, 64:]


def text_grads(ids, shares):
    tail = whole((TAIL, 128))
    return pl.pallas_call(
        text_kernel,
        grid=(1,),
        out_shape=(SDS((TXT_ROWS, 256), bf16), SDS((TXT_ROWS, 256), bf16), SDS((TXT, 64), bf16)),
        in_specs=[IN_SMEM] + [tail, tail, whole((TXT_PAD, 128))] * 2,
        out_specs=(whole((TXT_ROWS, 256)), whole((TXT_ROWS, 256)), whole((TXT, 64))),
        scratch_shapes=[pltpu.VMEM((TXT_PAD, 128), bf16)],
        name="text_grads",
        cost_estimate=cost(2),
        compiler_params=params(),
    )(ids, *shares)


def fold(x, n):
    lane = lax.broadcasted_iota(jnp.int32, (1, 128), 1)
    m = 2 * n - 128
    tail = jnp.where(lane < n + m, pltpu.roll(x[48:64], m, 1), pltpu.roll(x[64:80], 2 * m, 1))
    beside = jnp.concatenate([pltpu.roll(x[48:80], n, 1), tail], axis=0)
    return jnp.where(lane < n, x[:48], beside)


def unfold(x, n):
    lane = lax.broadcasted_iota(jnp.int32, (1, 128), 1)
    m = 2 * n - 128
    tail = jnp.concatenate([pltpu.roll(x[32:48], 128 - m, 1), pltpu.roll(x[32:48], 128 - 2 * m, 1)], axis=0)
    return jnp.concatenate([x, jnp.where(lane < 128 - n, pltpu.roll(x[:32], 128 - n, 1), tail)], axis=0)


def finish_last_kernel(ids_ref, y_in, got_ref, own_ref, other_ref, w_ref, w_other_ref, y_ref):
    y_ref[:, :TOK] = y_in[:, :TOK]
    add_shares(y_in.at[:, TOK : 2 * TOK], got_ref, y_ref.at[:, TOK : 2 * TOK])
    first = ids_ref[0] == 0
    n = w_ref.shape[2] // 4
    for r in range(w_ref.shape[0]):
        total = dot(own_ref[:, :192], w_ref[r], 1, 0) + dot(other_ref[:, :192], w_other_ref[r], 1, 0)
        for i in range(2):
            at = 2 * n * i
            piece = jnp.where(first, total[:, at : at + n], total[:, at + n : at + 2 * n])
            piece = jnp.concatenate([piece, jnp.zeros((TXT_ROWS, 128 - n), f32)], axis=1)
            y_ref[2 * ids_ref[1 + r] + i, 2 * TOK :] = fold(piece, n).astype(bf16)


def finish_last(ids, y, got, own, other, w, w_other):
    return pl.pallas_call(
        finish_last_kernel,
        out_shape=SDS(y.shape, bf16),
        in_specs=[IN_SMEM] + [IN_VMEM] * 6,
        out_specs=IN_VMEM,
        name="finish_last",
        cost_estimate=cost(5),
        compiler_params=params(),
    )(ids, y, got, own, other, w, w_other)


def unpack_kernel(z0_ref, z1_ref, o_ref, g_ref, dx_ref, acc):
    low = low_lanes()
    step = pl.program_id(0)
    total = jnp.zeros((DX_ROWS, 128), f32)
    for c in range(z0_ref.shape[0]):
        cols = slice(128 * c, 128 * c + 128)
        qo0, qo1 = z0_ref[c, :TOK], z1_ref[c, :TOK]
        kv0, kv1 = z0_ref[c, TOK : 2 * TOK], z1_ref[c, TOK : 2 * TOK]
        g_ref[0, :, cols] = jnp.where(low, qo0, swap(qo1))
        o_ref[:, cols] = jnp.where(low, swap(qo0), qo1)
        g_ref[1, :, cols] = jnp.where(low, kv0, swap(kv1))
        g_ref[2, :, cols] = jnp.where(low, swap(kv0), kv1)
        total += z1_ref[c, 2 * TOK :].astype(f32)

    @pl.when(step == 0)
    def _():
        acc[...] = total

    @pl.when(step > 0)
    def _():
        acc[...] += total

    @pl.when(step == pl.num_programs(0) - 1)
    def _():
        dx_ref[...] = unfold(acc[...], dx_ref.shape[0]).T[: dx_ref.shape[0], :TXT].reshape(dx_ref.shape)


def unpack(z0, z1, dx_cols):
    grid = 4
    width = 128 * CHIPS
    return pl.pallas_call(
        unpack_kernel,
        grid=(grid,),
        out_shape=(SDS((TOK, width), bf16), SDS((3, TOK, width), bf16), SDS((dx_cols, 1, TXT), f32)),
        in_specs=[pl.BlockSpec((CHIPS // grid, z.shape[1], 128), lambda i: (i, 0, 0)) for z in (z0, z1)],
        out_specs=(
            pl.BlockSpec((TOK, width // grid), lambda i: (0, i)),
            pl.BlockSpec((3, TOK, width // grid), lambda i: (0, 0, i)),
            whole((dx_cols, 1, TXT)),
        ),
        scratch_shapes=[pltpu.VMEM((DX_ROWS, 128), f32)],
        name="unpack",
        cost_estimate=cost(4),
        compiler_params=params(),
    )(z0, z1)


def weight_grad_kernel(x_ref, tg_ref, out_ref):
    total = jnp.zeros(out_ref.shape, f32)
    for r in range(x_ref.shape[0]):
        total += dot(tg_ref[r, :TXT, :192], x_ref[r], 0, 0)
    out_ref[...] = total


def weight_grad(x, tg):
    return pl.pallas_call(
        weight_grad_kernel,
        out_shape=SDS((192, x.shape[2]), f32),
        in_specs=[IN_VMEM] * 2,
        out_specs=IN_VMEM,
        name="weight_grad",
        cost_estimate=cost(4),
        compiler_params=params(),
    )(x, tg)


def local(q_img, k_img, v_img, x_txt, w_txt, grad_img, grad_txt):
    seq, dp = lax.axis_index("seq"), lax.axis_index("dp")
    core = seq % 2
    dp_hi, dp_lo = dp // 4, dp % 4
    pair = [(i, i ^ 1) for i in range(2 * CHIPS)]
    parity = [list(range(j, 2 * CHIPS, 2)) for j in range(2)]
    across = [(i, i ^ 4) for i in range(8)]
    turns = [[(i, i // 4 * 4 + (i + k) % 4) for i in range(8)] for k in range(1, 4)]

    def exchange(x):
        return lax.all_to_all(x, "seq", 0, 0, axis_index_groups=parity, tiled=True)

    def around(x, got):
        both = jnp.stack([x, got])
        return jnp.concatenate([both] + [lax.ppermute(both, "dp", t) for t in turns])

    order = [(dp_hi ^ side) * 4 + (dp_lo + 4 - k) % 4 for k in range(4) for side in range(2)]
    place = [2 * ((dp_lo + 4 - d % 4) % 4) + (dp_hi ^ (d // 4)) for d in range(8)]
    ids = jnp.stack([core] + order + place + [4 * (1 - dp_hi) + 2 * core]).astype(jnp.int32)
    image = (q_img[0], k_img[0], v_img[0], grad_img[0])

    w_own = jnp.swapaxes(w_txt, 1, 2).reshape(192, -1)
    w_across = lax.ppermute(w_own, "dp", across)

    packed = pack(0, *image, 4)
    packed, w_across = lax.optimization_barrier((packed, w_across))
    r0 = exchange(packed)
    weights = around(w_own, w_across)
    text, x8, half = project(ids, x_txt[0], weights, grad_txt[0])
    text_other = lax.ppermute(text, "seq", pair)
    weights_other = lax.ppermute(weights, "seq", pair)
    second = pack(1, *image, 4)
    r0, second, text_other, weights_other, half = lax.optimization_barrier(
        (r0, second, text_other, weights_other, half)
    )

    kv0 = lax.ppermute(r0[:, 1], "seq", pair)
    r1 = exchange(second)
    x_half = lax.ppermute(half, "dp", across)
    y0, ex0, dt0 = attend(0, ids, r0, kv0, text, text_other, 2 * TOK)
    ex0, x_half = lax.optimization_barrier((ex0, x_half))
    got0 = lax.ppermute(ex0, "seq", pair)
    kv1 = lax.ppermute(r1[:, 1], "seq", pair)
    z0 = exchange(finish_first(y0, got0))
    y1, ex1, dt1 = attend(1, ids, r1, kv1, text, text_other, 2 * TOK + DX_ROWS)
    got1 = lax.ppermute(ex1, "seq", pair)

    grads_own, grads_other, o_txt = text_grads(ids, (ex0, got0, dt0, ex1, got1, dt1))
    grads_across = lax.ppermute(grads_own, "dp", across)
    y1 = finish_last(ids, y1, got1, grads_own, grads_other, weights, weights_other)
    y1, grads_across, x_half = lax.optimization_barrier((y1, grads_across, x_half))
    z1 = exchange(y1)
    x_other = lax.ppermute(x_half, "seq", pair)
    x_across = jnp.where(core == 0, jnp.concatenate([x_half, x_other]), jnp.concatenate([x_other, x_half]))
    kept = lax.dynamic_slice_in_dim(x8, 4 * dp_hi, 4, 0)
    both = jnp.stack([kept, x_across], axis=1)
    columns = [lax.dynamic_index_in_dim(both, (dp_lo + k) % 4, 0, keepdims=False) for k in range(4)]
    x_all = jnp.concatenate([columns[0]] + [lax.ppermute(c, "dp", t) for c, t in zip(columns[1:], turns)])
    dw = weight_grad(x_all, around(grads_own, grads_across))
    dw = jnp.swapaxes(dw.reshape(3, 64, -1), 1, 2)
    o_img, grads, dx = unpack(z0, z1, x_txt.shape[2] // (2 * CHIPS))
    return o_img[None], o_txt[None], grads[:, None], dx.transpose(1, 2, 0), dw


def solution(mesh):
    in_specs = (
        P("dp", "seq", None),
        P("dp", "seq", None),
        P("dp", "seq", None),
        P("dp", None, None),
        P(None, "dp", "seq"),
        P("dp", "seq", None),
        P("dp", None, "seq"),
    )
    out_specs = (
        P("dp", "seq", None),
        P("dp", None, "seq"),
        P(None, "dp", "seq", None),
        P("dp", None, "seq"),
        P(None, "dp", "seq"),
    )
    return jax.shard_map(local, mesh=mesh, in_specs=in_specs, out_specs=out_specs, check_vma=False)
```

```python
import functools

import jax
import jax.numpy as jnp
from jax import lax
from jax.experimental import pallas as pl
from jax.experimental.pallas import tpu as pltpu
from jax.sharding import PartitionSpec as P

bf16, f32 = jnp.bfloat16, jnp.float32
SDS = jax.ShapeDtypeStruct
LOG2E = 1.4426950408889634
CHIPS = 16
TOK = 128
MINE = CHIPS * TOK
IMG = 2 * MINE
TXT = 77
TXT_ROWS = 80
TXT_PAD = 128
DX_ROWS = 48
TXT_HALF = TXT_PAD // 2
KEYS = IMG + TXT_PAD
STEPS = 4
SRC_STEP = CHIPS // STEPS
ROWS = SRC_STEP * TOK
TAIL = TXT_HALF + TXT_PAD
CHUNK = 512
VMEM = 40 << 20
IN_VMEM = pl.BlockSpec(memory_space=pltpu.VMEM)
IN_SMEM = pl.BlockSpec(memory_space=pltpu.SMEM)


def dot(a, b, ca, cb):
    return lax.dot_general(a, b, (((ca,), (cb,)), ((), ())), preferred_element_type=f32)


def low_lanes():
    return lax.broadcasted_iota(jnp.int32, (1, 128), 1) < 64


def swap(x):
    return jnp.concatenate([x[..., 64:], x[..., :64]], axis=-1)


def params(limit=VMEM):
    return pltpu.CompilerParams(vmem_limit_bytes=limit)


def whole(shape):
    return pl.BlockSpec(shape, lambda *i: (0,) * len(shape))


def cost(us):
    return pl.CostEstimate(flops=int(us * 1.15e9), bytes_accessed=1 << 20, transcendentals=0)


def pack_kernel(phase, q_ref, k_ref, v_ref, g_ref, x_ref):
    low = low_lanes()
    for c in range(q_ref.shape[1] // 128):
        cols = slice(128 * c, 128 * c + 128)
        q = q_ref[:, cols] * jnp.asarray(0.125, bf16)
        k, v, g = k_ref[:, cols], v_ref[:, cols], g_ref[:, cols]
        for which, (a, b) in enumerate(((q, g), (k, v))):
            if phase == 0:
                x_ref[c, which] = jnp.where(low, a, swap(b))
            else:
                x_ref[c, which] = jnp.where(low, swap(a), b)


def pack(phase, q, k, v, g, grid):
    part = pl.BlockSpec((TOK, q.shape[1] // grid), lambda i: (0, i))
    return pl.pallas_call(
        functools.partial(pack_kernel, phase),
        grid=(grid,),
        out_shape=SDS((CHIPS, 2, TOK, 128), bf16),
        in_specs=[part] * 4,
        out_specs=pl.BlockSpec((CHIPS // grid, 2, TOK, 128), lambda i: (i, 0, 0, 0)),
        name=("pack_first", "pack_second")[phase],
        cost_estimate=cost(3),
        compiler_params=params(60 << 20),
    )(q, k, v, g)


def project_kernel(ids_ref, x_ref, w_ref, g_ref, out_ref, x8_ref, half_ref):
    total = jnp.zeros((TXT, w_ref.shape[1]), f32)
    n = w_ref.shape[2]
    for d in range(w_ref.shape[0]):
        x = x_ref[:, n * d : n * d + n]
        x8_ref[d] = x
        total += dot(x, w_ref[ids_ref[9 + d]], 1, 1)
    for i in range(half_ref.shape[0]):
        half_ref[i] = x8_ref[ids_ref[17] + i]
    total = total.astype(bf16)
    q = total[:, :64] * jnp.asarray(0.125, bf16)
    out_ref[...] = jnp.zeros_like(out_ref)
    out_ref[0:TXT] = jnp.concatenate([q, g_ref[...]], axis=1)
    out_ref[TXT_PAD : TXT_PAD + TXT] = total[:, 64:]


def project(ids, x, w, g):
    return pl.pallas_call(
        project_kernel,
        out_shape=(
            SDS((2 * TXT_PAD, 128), bf16),
            SDS((w.shape[0], TXT, w.shape[2]), bf16),
            SDS((2, TXT, w.shape[2]), bf16),
        ),
        in_specs=[IN_SMEM] + [IN_VMEM] * 3,
        out_specs=(IN_VMEM,) * 3,
        name="project",
        cost_estimate=cost(3),
        compiler_params=params(),
    )(ids, x, w, g)


def key_chunks():
    return [(j, min(CHUNK, IMG - j)) for j in range(0, IMG, CHUNK)] + [(IMG, TXT_PAD)]


def attend_kernel(
    phase, ids_ref, q_ref, own_kv_ref, other_kv_ref, text_ref, text_other_ref, y_ref, ex_ref, dt_ref,
    keys, values, kvt, s_ref, e_ref, acc, tops,
):
    step = pl.program_id(0)
    core = ids_ref[0]
    mine = core == phase
    padding = lax.broadcasted_iota(jnp.int32, (1, TXT_PAD), 1) >= TXT
    chunks = key_chunks()

    def queries(i):
        return q_ref[pl.ds(SRC_STEP * i, SRC_STEP)].reshape(ROWS, 128)

    def score_parts(qg, slot):
        rows = qg.shape[0]
        q = qg[:, :64].astype(f32) * LOG2E
        q_high = q.astype(bf16)
        left = jnp.concatenate([q_high, (q - q_high.astype(f32)).astype(bf16)], axis=1)
        top = [jnp.full((rows, 128), -jnp.inf, f32)]

        def part(j, n):
            s = dot(left, keys[:, j : j + n], 1, 0)
            if j == IMG:
                s = jnp.where(padding, -jnp.inf, s)
            s_ref[slot, :rows, j : j + n] = s
            for i in range(0, n, 128):
                top[0] = jnp.maximum(top[0], s[:, i : i + 128])

        def last():
            tops[slot, :rows] = jnp.broadcast_to(jnp.max(top[0], axis=1, keepdims=True), (rows, 128))

        return part, last

    @pl.when(step == 0)
    def _():
        text = jnp.where(mine, text_ref[TXT_PAD:], text_other_ref[TXT_PAD:])
        for j, n, x in ((0, MINE, own_kv_ref), (MINE, MINE, other_kv_ref), (IMG, TXT_PAD, None)):
            t = (text if x is None else x[...].reshape(n, 128)).T
            cols = slice(j, j + n)
            kvt[0:128, cols] = t
            keys[0:64, cols] = t[:64]
            keys[64:128, cols] = t[:64]
            minus = lax.broadcasted_iota(jnp.int32, (64, n), 0) < 2
            values[0:64, cols] = jnp.where(minus, -1.0, 0.0).astype(bf16)
            values[64:128, cols] = t[64:]
        kvt[128:144] = jnp.ones((16, KEYS), bf16)
        acc[...] = jnp.zeros_like(acc)
        part, last = score_parts(queries(0), 0)
        for j, n in chunks:
            part(j, n)
        last()

    def block(qg, slot, following=None):
        rows = qg.shape[0]
        qgt = qg.T
        top = tops[slot, :rows, 0:1]
        ot = jnp.zeros((80, rows), f32)
        part, last = score_parts(following, 1 - slot) if following is not None else (None, None)
        for j, n in chunks:
            e = jnp.exp2(s_ref[slot, :rows, j : j + n] - top).astype(bf16)
            e_ref[:rows, j : j + n] = e
            if part:
                part(j, n)
            ot = ot + dot(kvt[64:144, j : j + n], e, 1, 1)
        if last:
            last()
        inv = 1.0 / ot[64:65]
        ot = (ot[:64] * inv).astype(bf16).astype(f32)
        gt = qgt[64:].astype(f32)
        row_term = jnp.sum(gt * ot, axis=0, keepdims=True) * inv
        gt = (gt * inv).astype(bf16)
        high = row_term.astype(bf16).astype(f32)
        left = jnp.concatenate([high, row_term - high, jnp.zeros((62, rows), f32), gt.astype(f32)], axis=0)
        left = left.astype(bf16).T
        dqt = jnp.zeros((64, rows), f32)

        def prob_grads(k):
            return dot(left, values[:, chunks[k][0] : chunks[k][0] + chunks[k][1]], 1, 0)

        dp = prob_grads(0)
        for k, (j, n) in enumerate(chunks):
            e = e_ref[:rows, j : j + n]
            ds = e * dp.astype(bf16)
            if k + 1 < len(chunks):
                dp = prob_grads(k + 1)
            dqt = dqt + dot(kvt[0:64, j : j + n], ds, 1, 1)
            acc[0:64, j : j + n] += dot(qgt[0:64], ds, 1, 0)
            acc[64:128, j : j + n] += dot(gt, e, 1, 0)
        return jnp.concatenate([dqt * 0.125, ot], axis=0).T.astype(bf16)

    def store(i, r):
        y_ref[pl.ds(SRC_STEP * i, SRC_STEP), :TOK] = r.reshape(SRC_STEP, TOK, 128)

    @pl.when(step % 2 == 0)
    def _():
        store(step, block(queries(step), 0, queries(step + 1)))

    @pl.when(step == 1)
    def _():
        store(1, block(queries(1), 1, queries(2)))

    @pl.when(step == STEPS - 1)
    def _():
        rows = pl.ds(pl.multiple_of(TXT_HALF * core, TXT_HALF), TXT_HALF)
        text = jnp.where(mine, text_ref[rows], text_other_ref[rows])
        store(STEPS - 1, block(queries(STEPS - 1), 1, text))
        ex_ref[:TXT_HALF] = block(text, 0)
        dt = acc[:, IMG:].T
        dt_ref[...] = dt
        ex_ref[TXT_HALF:TAIL] = dt.astype(bf16)
        ex_ref[TAIL:] = acc[:, MINE:IMG].T.astype(bf16)
        y_ref[:, TOK : 2 * TOK] = acc[:, :MINE].T.astype(bf16).reshape(CHIPS, TOK, 128)


def attend(phase, ids, received, other, text, text_other, y_rows):
    half = (CHIPS, TOK, 128)
    text_shape = (2 * TXT_PAD, 128)
    return pl.pallas_call(
        functools.partial(attend_kernel, phase),
        grid=(STEPS,),
        out_shape=(
            SDS((CHIPS, y_rows, 128), bf16),
            SDS((TAIL + MINE, 128), bf16),
            SDS((TXT_PAD, 128), f32),
        ),
        in_specs=[
            IN_SMEM,
            pl.BlockSpec((CHIPS, None, TOK, 128), lambda i: (0, 0, 0, 0)),
            pl.BlockSpec((CHIPS, None, TOK, 128), lambda i: (0, 1, 0, 0)),
            whole(half),
            whole(text_shape),
            whole(text_shape),
        ],
        out_specs=(whole((CHIPS, y_rows, 128)), whole((TAIL + MINE, 128)), whole((TXT_PAD, 128))),
        scratch_shapes=[
            pltpu.VMEM((128, KEYS), bf16),
            pltpu.VMEM((128, KEYS), bf16),
            pltpu.VMEM((144, KEYS), bf16),
            pltpu.VMEM((2, ROWS, KEYS), f32),
            pltpu.VMEM((ROWS, KEYS), bf16),
            pltpu.VMEM((128, KEYS), f32),
            pltpu.VMEM((2, ROWS, 128), f32),
        ],
        name=("attend_first", "attend_second")[phase],
        cost_estimate=cost(32),
        compiler_params=params(60 << 20),
    )(ids, received, received, other, text, text_other)


def add_shares(y_in, got_ref, y_ref):
    for i in range(CHIPS):
        got = got_ref[TAIL + TOK * i : TAIL + TOK * i + TOK].astype(f32)
        y_ref[i] = (y_in[i].astype(f32) + got).astype(bf16)


def finish_first(y, got):
    part = pl.BlockSpec((CHIPS, TOK, 128), lambda i: (0, 1, 0))
    return pl.pallas_call(
        add_shares,
        grid=(1,),
        out_shape=SDS(y.shape, bf16),
        in_specs=[part, whole(got.shape)],
        out_specs=part,
        input_output_aliases={0: 0},
        name="finish_first",
        cost_estimate=cost(2),
        compiler_params=params(60 << 20),
    )(y, got)


def text_kernel(ids_ref, ex0_ref, got0_ref, dt0_ref, ex1_ref, got1_ref, dt1_ref, own_ref, other_ref, o_ref, rows_ref):
    core = ids_ref[0]
    low = low_lanes()
    heads = []
    for ex, got, dt in ((ex0_ref, got0_ref, dt0_ref), (ex1_ref, got1_ref, dt1_ref)):
        rows_ref[pl.ds(pl.multiple_of(TXT_HALF * core, TXT_HALF), TXT_HALF)] = ex[:TXT_HALF]
        rows_ref[pl.ds(pl.multiple_of(TXT_HALF * (1 - core), TXT_HALF), TXT_HALF)] = got[:TXT_HALF]
        qo = rows_ref[0:TXT_ROWS]
        kv = (dt[...] + got[TXT_HALF:TAIL].astype(f32)).astype(bf16)[:TXT_ROWS]
        heads.append((qo, kv))
    for target, which in ((own_ref, core == 0), (other_ref, core == 1)):
        qo, kv = (jnp.where(which, a, b) for a, b in zip(*heads))
        vk = swap(kv)
        target[:, :128] = jnp.where(low, qo, vk)
        target[:, 128:] = jnp.where(low, vk, jnp.zeros_like(vk))
        if target is own_ref:
            o_ref[...] = qo[:TXT, 64:]


def text_grads(ids, shares):
    tail = whole((TAIL, 128))
    return pl.pallas_call(
        text_kernel,
        grid=(1,),
        out_shape=(SDS((TXT_ROWS, 256), bf16), SDS((TXT_ROWS, 256), bf16), SDS((TXT, 64), bf16)),
        in_specs=[IN_SMEM] + [tail, tail, whole((TXT_PAD, 128))] * 2,
        out_specs=(whole((TXT_ROWS, 256)), whole((TXT_ROWS, 256)), whole((TXT, 64))),
        scratch_shapes=[pltpu.VMEM((TXT_PAD, 128), bf16)],
        name="text_grads",
        cost_estimate=cost(2),
        compiler_params=params(),
    )(ids, *shares)


def fold(x, n):
    lane = lax.broadcasted_iota(jnp.int32, (1, 128), 1)
    m = 2 * n - 128
    tail = jnp.where(lane < n + m, pltpu.roll(x[48:64], m, 1), pltpu.roll(x[64:80], 2 * m, 1))
    beside = jnp.concatenate([pltpu.roll(x[48:80], n, 1), tail], axis=0)
    return jnp.where(lane < n, x[:48], beside)


def unfold(x, n):
    lane = lax.broadcasted_iota(jnp.int32, (1, 128), 1)
    m = 2 * n - 128
    tail = jnp.concatenate([pltpu.roll(x[32:48], 128 - m, 1), pltpu.roll(x[32:48], 128 - 2 * m, 1)], axis=0)
    return jnp.concatenate([x, jnp.where(lane < 128 - n, pltpu.roll(x[:32], 128 - n, 1), tail)], axis=0)


def finish_last_kernel(ids_ref, y_in, got_ref, own_ref, other_ref, w_ref, w_other_ref, y_ref):
    y_ref[:, :TOK] = y_in[:, :TOK]
    add_shares(y_in.at[:, TOK : 2 * TOK], got_ref, y_ref.at[:, TOK : 2 * TOK])
    first = ids_ref[0] == 0
    n = w_ref.shape[2] // 4
    for r in range(w_ref.shape[0]):
        total = dot(own_ref[:, :192], w_ref[r], 1, 0) + dot(other_ref[:, :192], w_other_ref[r], 1, 0)
        for i in range(2):
            at = 2 * n * i
            piece = jnp.where(first, total[:, at : at + n], total[:, at + n : at + 2 * n])
            piece = jnp.concatenate([piece, jnp.zeros((TXT_ROWS, 128 - n), f32)], axis=1)
            y_ref[2 * ids_ref[1 + r] + i, 2 * TOK :] = fold(piece, n).astype(bf16)


def finish_last(ids, y, got, own, other, w, w_other):
    return pl.pallas_call(
        finish_last_kernel,
        out_shape=SDS(y.shape, bf16),
        in_specs=[IN_SMEM] + [IN_VMEM] * 6,
        out_specs=IN_VMEM,
        name="finish_last",
        cost_estimate=cost(5),
        compiler_params=params(),
    )(ids, y, got, own, other, w, w_other)


def unpack_kernel(z0_ref, z1_ref, o_ref, g_ref, dx_ref, acc):
    low = low_lanes()
    step = pl.program_id(0)
    total = jnp.zeros((DX_ROWS, 128), f32)
    for c in range(z0_ref.shape[0]):
        cols = slice(128 * c, 128 * c + 128)
        qo0, qo1 = z0_ref[c, :TOK], z1_ref[c, :TOK]
        kv0, kv1 = z0_ref[c, TOK : 2 * TOK], z1_ref[c, TOK : 2 * TOK]
        g_ref[0, :, cols] = jnp.where(low, qo0, swap(qo1))
        o_ref[:, cols] = jnp.where(low, swap(qo0), qo1)
        g_ref[1, :, cols] = jnp.where(low, kv0, swap(kv1))
        g_ref[2, :, cols] = jnp.where(low, swap(kv0), kv1)
        total += z1_ref[c, 2 * TOK :].astype(f32)

    @pl.when(step == 0)
    def _():
        acc[...] = total

    @pl.when(step > 0)
    def _():
        acc[...] += total

    @pl.when(step == pl.num_programs(0) - 1)
    def _():
        dx_ref[...] = unfold(acc[...], dx_ref.shape[0]).T[: dx_ref.shape[0], :TXT].reshape(dx_ref.shape)


def unpack(z0, z1, dx_cols):
    grid = 4
    width = 128 * CHIPS
    return pl.pallas_call(
        unpack_kernel,
        grid=(grid,),
        out_shape=(SDS((TOK, width), bf16), SDS((3, TOK, width), bf16), SDS((dx_cols, 1, TXT), f32)),
        in_specs=[pl.BlockSpec((CHIPS // grid, z.shape[1], 128), lambda i: (i, 0, 0)) for z in (z0, z1)],
        out_specs=(
            pl.BlockSpec((TOK, width // grid), lambda i: (0, i)),
            pl.BlockSpec((3, TOK, width // grid), lambda i: (0, 0, i)),
            whole((dx_cols, 1, TXT)),
        ),
        scratch_shapes=[pltpu.VMEM((DX_ROWS, 128), f32)],
        name="unpack",
        cost_estimate=cost(4),
        compiler_params=params(),
    )(z0, z1)


def weight_grad_kernel(x_ref, tg_ref, out_ref):
    total = jnp.zeros(out_ref.shape, f32)
    for r in range(x_ref.shape[0]):
        total += dot(tg_ref[r, :TXT, :192], x_ref[r], 0, 0)
    out_ref[...] = total


def weight_grad(x, tg):
    return pl.pallas_call(
        weight_grad_kernel,
        out_shape=SDS((192, x.shape[2]), f32),
        in_specs=[IN_VMEM] * 2,
        out_specs=IN_VMEM,
        name="weight_grad",
        cost_estimate=cost(4),
        compiler_params=params(),
    )(x, tg)


def local(q_img, k_img, v_img, x_txt, w_txt, grad_img, grad_txt):
    seq, dp = lax.axis_index("seq"), lax.axis_index("dp")
    core = seq % 2
    dp_hi, dp_lo = dp // 4, dp % 4
    pair = [(i, i ^ 1) for i in range(2 * CHIPS)]
    parity = [list(range(j, 2 * CHIPS, 2)) for j in range(2)]
    across = [(i, i ^ 4) for i in range(8)]
    turns = [[(i, i // 4 * 4 + (i + k) % 4) for i in range(8)] for k in range(1, 4)]

    def exchange(x):
        return lax.all_to_all(x, "seq", 0, 0, axis_index_groups=parity, tiled=True)

    def around(x, got):
        both = jnp.stack([x, got])
        return jnp.concatenate([both] + [lax.ppermute(both, "dp", t) for t in turns])

    order = [(dp_hi ^ side) * 4 + (dp_lo + 4 - k) % 4 for k in range(4) for side in range(2)]
    place = [2 * ((dp_lo + 4 - d % 4) % 4) + (dp_hi ^ (d // 4)) for d in range(8)]
    ids = jnp.stack([core] + order + place + [4 * (1 - dp_hi) + 2 * core]).astype(jnp.int32)
    image = (q_img[0], k_img[0], v_img[0], grad_img[0])

    w_own = jnp.swapaxes(w_txt, 1, 2).reshape(192, -1)
    w_across = lax.ppermute(w_own, "dp", across)

    packed = pack(0, *image, 4)
    packed, w_across = lax.optimization_barrier((packed, w_across))
    r0 = exchange(packed)
    weights = around(w_own, w_across)
    text, x8, half = project(ids, x_txt[0], weights, grad_txt[0])
    text_other = lax.ppermute(text, "seq", pair)
    weights_other = lax.ppermute(weights, "seq", pair)
    second = pack(1, *image, 4)
    r0, second, text_other, weights_other, half = lax.optimization_barrier(
        (r0, second, text_other, weights_other, half)
    )

    kv0 = lax.ppermute(r0[:, 1], "seq", pair)
    r1 = exchange(second)
    x_half = lax.ppermute(half, "dp", across)
    y0, ex0, dt0 = attend(0, ids, r0, kv0, text, text_other, 2 * TOK)
    ex0, x_half = lax.optimization_barrier((ex0, x_half))
    got0 = lax.ppermute(ex0, "seq", pair)
    kv1 = lax.ppermute(r1[:, 1], "seq", pair)
    z0 = exchange(finish_first(y0, got0))
    y1, ex1, dt1 = attend(1, ids, r1, kv1, text, text_other, 2 * TOK + DX_ROWS)
    got1 = lax.ppermute(ex1, "seq", pair)

    grads_own, grads_other, o_txt = text_grads(ids, (ex0, got0, dt0, ex1, got1, dt1))
    grads_across = lax.ppermute(grads_own, "dp", across)
    y1 = finish_last(ids, y1, got1, grads_own, grads_other, weights, weights_other)
    y1, grads_across, x_half = lax.optimization_barrier((y1, grads_across, x_half))
    z1 = exchange(y1)
    x_other = lax.ppermute(x_half, "seq", pair)
    x_across = jnp.where(core == 0, jnp.concatenate([x_half, x_other]), jnp.concatenate([x_other, x_half]))
    kept = lax.dynamic_slice_in_dim(x8, 4 * dp_hi, 4, 0)
    both = jnp.stack([kept, x_across], axis=1)
    columns = [lax.dynamic_index_in_dim(both, (dp_lo + k) % 4, 0, keepdims=False) for k in range(4)]
    x_all = jnp.concatenate([columns[0]] + [lax.ppermute(c, "dp", t) for c, t in zip(columns[1:], turns)])
    dw = weight_grad(x_all, around(grads_own, grads_across))
    dw = jnp.swapaxes(dw.reshape(3, 64, -1), 1, 2)
    o_img, grads, dx = unpack(z0, z1, x_txt.shape[2] // (2 * CHIPS))
    return o_img[None], o_txt[None], grads[:, None], dx.transpose(1, 2, 0), dw


def solution(mesh):
    in_specs = (
        P("dp", "seq", None),
        P("dp", "seq", None),
        P("dp", "seq", None),
        P("dp", None, None),
        P(None, "dp", "seq"),
        P("dp", "seq", None),
        P("dp", None, "seq"),
    )
    out_specs = (
        P("dp", "seq", None),
        P("dp", None, "seq"),
        P(None, "dp", "seq", None),
        P("dp", None, "seq"),
        P(None, "dp", "seq"),
    )
    return jax.shard_map(local, mesh=mesh, in_specs=in_specs, out_specs=out_specs, check_vma=False)
```

```python
import functools

import jax
import jax.numpy as jnp
from jax import lax
from jax.experimental import pallas as pl
from jax.experimental.pallas import tpu as pltpu
from jax.sharding import PartitionSpec as P

bf16, f32 = jnp.bfloat16, jnp.float32
SDS = jax.ShapeDtypeStruct
LOG2E = 1.4426950408889634
CHIPS = 16
TOK = 128
MINE = CHIPS * TOK
IMG = 2 * MINE
TXT = 77
TXT_ROWS = 80
TXT_PAD = 128
DX_ROWS = 48
TXT_HALF = TXT_PAD // 2
KEYS = IMG + TXT_PAD
STEPS = 4
SRC_STEP = CHIPS // STEPS
ROWS = SRC_STEP * TOK
TAIL = TXT_HALF + TXT_PAD
CHUNK = 1024
VMEM = 40 << 20
IN_VMEM = pl.BlockSpec(memory_space=pltpu.VMEM)
IN_SMEM = pl.BlockSpec(memory_space=pltpu.SMEM)


def dot(a, b, ca, cb):
    return lax.dot_general(a, b, (((ca,), (cb,)), ((), ())), preferred_element_type=f32)


def low_lanes():
    return lax.broadcasted_iota(jnp.int32, (1, 128), 1) < 64


def swap(x):
    return jnp.concatenate([x[..., 64:], x[..., :64]], axis=-1)


def params(limit=VMEM):
    return pltpu.CompilerParams(vmem_limit_bytes=limit)


def whole(shape):
    return pl.BlockSpec(shape, lambda *i: (0,) * len(shape))


def cost(us):
    return pl.CostEstimate(flops=int(us * 1.15e9), bytes_accessed=1 << 20, transcendentals=0)


def pack_kernel(phase, q_ref, k_ref, v_ref, g_ref, x_ref):
    low = low_lanes()
    for c in range(q_ref.shape[1] // 128):
        cols = slice(128 * c, 128 * c + 128)
        q = q_ref[:, cols] * jnp.asarray(0.125, bf16)
        k, v, g = k_ref[:, cols], v_ref[:, cols], g_ref[:, cols]
        for which, (a, b) in enumerate(((q, g), (k, v))):
            if phase == 0:
                x_ref[c, which] = jnp.where(low, a, swap(b))
            else:
                x_ref[c, which] = jnp.where(low, swap(a), b)


def pack(phase, q, k, v, g, grid):
    part = pl.BlockSpec((TOK, q.shape[1] // grid), lambda i: (0, i))
    return pl.pallas_call(
        functools.partial(pack_kernel, phase),
        grid=(grid,),
        out_shape=SDS((CHIPS, 2, TOK, 128), bf16),
        in_specs=[part] * 4,
        out_specs=pl.BlockSpec((CHIPS // grid, 2, TOK, 128), lambda i: (i, 0, 0, 0)),
        name=("pack_first", "pack_second")[phase],
        cost_estimate=cost(3),
        compiler_params=params(60 << 20),
    )(q, k, v, g)


def project_kernel(ids_ref, x_ref, w_ref, g_ref, out_ref, x8_ref, half_ref):
    total = jnp.zeros((TXT, w_ref.shape[1]), f32)
    n = w_ref.shape[2]
    for d in range(w_ref.shape[0]):
        x = x_ref[:, n * d : n * d + n]
        x8_ref[d] = x
        total += dot(x, w_ref[ids_ref[9 + d]], 1, 1)
    for i in range(half_ref.shape[0]):
        half_ref[i] = x8_ref[ids_ref[17] + i]
    total = total.astype(bf16)
    q = total[:, :64] * jnp.asarray(0.125, bf16)
    out_ref[...] = jnp.zeros_like(out_ref)
    out_ref[0:TXT] = jnp.concatenate([q, g_ref[...]], axis=1)
    out_ref[TXT_PAD : TXT_PAD + TXT] = total[:, 64:]


def project(ids, x, w, g):
    return pl.pallas_call(
        project_kernel,
        out_shape=(
            SDS((2 * TXT_PAD, 128), bf16),
            SDS((w.shape[0], TXT, w.shape[2]), bf16),
            SDS((2, TXT, w.shape[2]), bf16),
        ),
        in_specs=[IN_SMEM] + [IN_VMEM] * 3,
        out_specs=(IN_VMEM,) * 3,
        name="project",
        cost_estimate=cost(3),
        compiler_params=params(),
    )(ids, x, w, g)


def key_chunks():
    return [(j, min(CHUNK, IMG - j)) for j in range(0, IMG, CHUNK)] + [(IMG, TXT_PAD)]


def attend_kernel(
    phase, ids_ref, q_ref, own_kv_ref, other_kv_ref, text_ref, text_other_ref, y_ref, ex_ref, dt_ref,
    keys, values, kvt, s_ref, e_ref, acc,
):
    step = pl.program_id(0)
    core = ids_ref[0]
    mine = core == phase

    @pl.when(step == 0)
    def _():
        text = jnp.where(mine, text_ref[TXT_PAD:], text_other_ref[TXT_PAD:])
        for j, n, x in ((0, MINE, own_kv_ref), (MINE, MINE, other_kv_ref), (IMG, TXT_PAD, None)):
            t = (text if x is None else x[...].reshape(n, 128)).T
            cols = slice(j, j + n)
            kvt[0:128, cols] = t
            keys[0:64, cols] = t[:64]
            keys[64:128, cols] = t[:64]
            minus = lax.broadcasted_iota(jnp.int32, (64, n), 0) < 2
            values[0:64, cols] = jnp.where(minus, -1.0, 0.0).astype(bf16)
            values[64:128, cols] = t[64:]
        kvt[128:144] = jnp.ones((16, KEYS), bf16)
        acc[...] = jnp.zeros_like(acc)

    padding = lax.broadcasted_iota(jnp.int32, (1, TXT_PAD), 1) >= TXT

    def block(qg):
        rows = qg.shape[0]
        qgt = qg.T
        q = qg[:, :64].astype(f32) * LOG2E
        q_high = q.astype(bf16)
        left = jnp.concatenate([q_high, (q - q_high.astype(f32)).astype(bf16)], axis=1)
        top = jnp.full((rows, 128), -jnp.inf, f32)
        for j, n in key_chunks():
            s = dot(left, keys[:, j : j + n], 1, 0)
            if j == IMG:
                s = jnp.where(padding, -jnp.inf, s)
            s_ref[:rows, j : j + n] = s
            for i in range(0, n, 128):
                top = jnp.maximum(top, s[:, i : i + 128])
        top = jnp.max(top, axis=1, keepdims=True)
        ot = jnp.zeros((80, rows), f32)
        for j, n in key_chunks():
            e = jnp.exp2(s_ref[:rows, j : j + n] - top).astype(bf16)
            e_ref[:rows, j : j + n] = e
            ot = ot + dot(kvt[64:144, j : j + n], e, 1, 1)
        inv = 1.0 / ot[64:65]
        ot = (ot[:64] * inv).astype(bf16).astype(f32)
        gt = qgt[64:].astype(f32)
        row_term = jnp.sum(gt * ot, axis=0, keepdims=True) * inv
        gt = (gt * inv).astype(bf16)
        high = row_term.astype(bf16).astype(f32)
        left = jnp.concatenate([high, row_term - high, jnp.zeros((62, rows), f32), gt.astype(f32)], axis=0)
        left = left.astype(bf16).T
        dqt = jnp.zeros((64, rows), f32)
        chunks = key_chunks()

        def prob_grads(k):
            return dot(left, values[:, chunks[k][0] : chunks[k][0] + chunks[k][1]], 1, 0)

        dp = prob_grads(0)
        for k, (j, n) in enumerate(chunks):
            e = e_ref[:rows, j : j + n]
            ds = e * dp.astype(bf16)
            if k + 1 < len(chunks):
                dp = prob_grads(k + 1)
            dqt = dqt + dot(kvt[0:64, j : j + n], ds, 1, 1)
            acc[0:64, j : j + n] += dot(qgt[0:64], ds, 1, 0)
            acc[64:128, j : j + n] += dot(gt, e, 1, 0)
        return jnp.concatenate([dqt * 0.125, ot], axis=0).T.astype(bf16)

    y_ref[pl.ds(SRC_STEP * step, SRC_STEP), :TOK] = block(q_ref[...].reshape(ROWS, 128)).reshape(SRC_STEP, TOK, 128)

    @pl.when(step == STEPS - 1)
    def _():
        rows = pl.ds(pl.multiple_of(TXT_HALF * core, TXT_HALF), TXT_HALF)
        ex_ref[:TXT_HALF] = block(jnp.where(mine, text_ref[rows], text_other_ref[rows]))
        dt = acc[:, IMG:].T
        dt_ref[...] = dt
        ex_ref[TXT_HALF:TAIL] = dt.astype(bf16)
        ex_ref[TAIL:] = acc[:, MINE:IMG].T.astype(bf16)
        y_ref[:, TOK : 2 * TOK] = acc[:, :MINE].T.astype(bf16).reshape(CHIPS, TOK, 128)


def attend(phase, ids, received, other, text, text_other, y_rows):
    return pl.pallas_call(
        functools.partial(attend_kernel, phase),
        grid=(STEPS,),
        out_shape=(
            SDS((CHIPS, y_rows, 128), bf16),
            SDS((TAIL + MINE, 128), bf16),
            SDS((TXT_PAD, 128), f32),
        ),
        in_specs=[
            IN_SMEM,
            pl.BlockSpec((SRC_STEP, None, TOK, 128), lambda i: (i, 0, 0, 0)),
            pl.BlockSpec((CHIPS, None, TOK, 128), lambda i: (0, 1, 0, 0)),
            IN_VMEM,
            IN_VMEM,
            IN_VMEM,
        ],
        out_specs=(whole((CHIPS, y_rows, 128)), whole((TAIL + MINE, 128)), whole((TXT_PAD, 128))),
        scratch_shapes=[
            pltpu.VMEM((128, KEYS), bf16),
            pltpu.VMEM((128, KEYS), bf16),
            pltpu.VMEM((144, KEYS), bf16),
            pltpu.VMEM((ROWS, KEYS), f32),
            pltpu.VMEM((ROWS, KEYS), bf16),
            pltpu.VMEM((128, KEYS), f32),
        ],
        name=("attend_first", "attend_second")[phase],
        cost_estimate=cost(34),
        compiler_params=params(),
    )(ids, received, received, other, text, text_other)


def add_shares(y_in, got_ref, y_ref):
    for i in range(CHIPS):
        got = got_ref[TAIL + TOK * i : TAIL + TOK * i + TOK].astype(f32)
        y_ref[i] = (y_in[i].astype(f32) + got).astype(bf16)


def finish_first_kernel(y_in, got_ref, y_ref):
    y_ref[:, :TOK] = y_in[:, :TOK]
    add_shares(y_in.at[:, TOK:], got_ref, y_ref.at[:, TOK:])


def finish_first(y, got):
    return pl.pallas_call(
        finish_first_kernel,
        out_shape=SDS(y.shape, bf16),
        in_specs=[IN_VMEM] * 2,
        out_specs=IN_VMEM,
        name="finish_first",
        cost_estimate=cost(2),
        compiler_params=params(),
    )(y, got)


def text_kernel(ids_ref, ex0_ref, got0_ref, dt0_ref, ex1_ref, got1_ref, dt1_ref, own_ref, other_ref, o_ref, rows_ref):
    core = ids_ref[0]
    low = low_lanes()
    heads = []
    for ex, got, dt in ((ex0_ref, got0_ref, dt0_ref), (ex1_ref, got1_ref, dt1_ref)):
        rows_ref[pl.ds(pl.multiple_of(TXT_HALF * core, TXT_HALF), TXT_HALF)] = ex[:TXT_HALF]
        rows_ref[pl.ds(pl.multiple_of(TXT_HALF * (1 - core), TXT_HALF), TXT_HALF)] = got[:TXT_HALF]
        qo = rows_ref[0:TXT_ROWS]
        kv = (dt[...] + got[TXT_HALF:TAIL].astype(f32)).astype(bf16)[:TXT_ROWS]
        heads.append((qo, kv))
    for target, which in ((own_ref, core == 0), (other_ref, core == 1)):
        qo, kv = (jnp.where(which, a, b) for a, b in zip(*heads))
        vk = swap(kv)
        target[:, :128] = jnp.where(low, qo, vk)
        target[:, 128:] = jnp.where(low, vk, jnp.zeros_like(vk))
        if target is own_ref:
            o_ref[...] = qo[:TXT, 64:]


def text_grads(ids, shares):
    tail = whole((TAIL, 128))
    return pl.pallas_call(
        text_kernel,
        grid=(1,),
        out_shape=(SDS((TXT_ROWS, 256), bf16), SDS((TXT_ROWS, 256), bf16), SDS((TXT, 64), bf16)),
        in_specs=[IN_SMEM] + [tail, tail, whole((TXT_PAD, 128))] * 2,
        out_specs=(whole((TXT_ROWS, 256)), whole((TXT_ROWS, 256)), whole((TXT, 64))),
        scratch_shapes=[pltpu.VMEM((TXT_PAD, 128), bf16)],
        name="text_grads",
        cost_estimate=cost(2),
        compiler_params=params(),
    )(ids, *shares)


def fold(x, n):
    lane = lax.broadcasted_iota(jnp.int32, (1, 128), 1)
    m = 2 * n - 128
    tail = jnp.where(lane < n + m, pltpu.roll(x[48:64], m, 1), pltpu.roll(x[64:80], 2 * m, 1))
    beside = jnp.concatenate([pltpu.roll(x[48:80], n, 1), tail], axis=0)
    return jnp.where(lane < n, x[:48], beside)


def unfold(x, n):
    lane = lax.broadcasted_iota(jnp.int32, (1, 128), 1)
    m = 2 * n - 128
    tail = jnp.concatenate([pltpu.roll(x[32:48], 128 - m, 1), pltpu.roll(x[32:48], 128 - 2 * m, 1)], axis=0)
    return jnp.concatenate([x, jnp.where(lane < 128 - n, pltpu.roll(x[:32], 128 - n, 1), tail)], axis=0)


def finish_last_kernel(ids_ref, y_in, got_ref, own_ref, other_ref, w_ref, w_other_ref, y_ref):
    y_ref[:, :TOK] = y_in[:, :TOK]
    add_shares(y_in.at[:, TOK : 2 * TOK], got_ref, y_ref.at[:, TOK : 2 * TOK])
    first = ids_ref[0] == 0
    n = w_ref.shape[2] // 4
    for r in range(w_ref.shape[0]):
        total = dot(own_ref[:, :192], w_ref[r], 1, 0) + dot(other_ref[:, :192], w_other_ref[r], 1, 0)
        for i in range(2):
            at = 2 * n * i
            piece = jnp.where(first, total[:, at : at + n], total[:, at + n : at + 2 * n])
            piece = jnp.concatenate([piece, jnp.zeros((TXT_ROWS, 128 - n), f32)], axis=1)
            y_ref[2 * ids_ref[1 + r] + i, 2 * TOK :] = fold(piece, n).astype(bf16)


def finish_last(ids, y, got, own, other, w, w_other):
    return pl.pallas_call(
        finish_last_kernel,
        out_shape=SDS(y.shape, bf16),
        in_specs=[IN_SMEM] + [IN_VMEM] * 6,
        out_specs=IN_VMEM,
        name="finish_last",
        cost_estimate=cost(5),
        compiler_params=params(),
    )(ids, y, got, own, other, w, w_other)


def unpack_kernel(z0_ref, z1_ref, o_ref, g_ref, dx_ref, acc):
    low = low_lanes()
    step = pl.program_id(0)
    total = jnp.zeros((DX_ROWS, 128), f32)
    for c in range(z0_ref.shape[0]):
        cols = slice(128 * c, 128 * c + 128)
        qo0, qo1 = z0_ref[c, :TOK], z1_ref[c, :TOK]
        kv0, kv1 = z0_ref[c, TOK : 2 * TOK], z1_ref[c, TOK : 2 * TOK]
        g_ref[0, :, cols] = jnp.where(low, qo0, swap(qo1))
        o_ref[:, cols] = jnp.where(low, swap(qo0), qo1)
        g_ref[1, :, cols] = jnp.where(low, kv0, swap(kv1))
        g_ref[2, :, cols] = jnp.where(low, swap(kv0), kv1)
        total += z1_ref[c, 2 * TOK :].astype(f32)

    @pl.when(step == 0)
    def _():
        acc[...] = total

    @pl.when(step > 0)
    def _():
        acc[...] += total

    @pl.when(step == pl.num_programs(0) - 1)
    def _():
        dx_ref[...] = unfold(acc[...], dx_ref.shape[0]).T[: dx_ref.shape[0], :TXT].reshape(dx_ref.shape)


def unpack(z0, z1, dx_cols):
    grid = 4
    width = 128 * CHIPS
    return pl.pallas_call(
        unpack_kernel,
        grid=(grid,),
        out_shape=(SDS((TOK, width), bf16), SDS((3, TOK, width), bf16), SDS((dx_cols, 1, TXT), f32)),
        in_specs=[pl.BlockSpec((CHIPS // grid, z.shape[1], 128), lambda i: (i, 0, 0)) for z in (z0, z1)],
        out_specs=(
            pl.BlockSpec((TOK, width // grid), lambda i: (0, i)),
            pl.BlockSpec((3, TOK, width // grid), lambda i: (0, 0, i)),
            whole((dx_cols, 1, TXT)),
        ),
        scratch_shapes=[pltpu.VMEM((DX_ROWS, 128), f32)],
        name="unpack",
        cost_estimate=cost(4),
        compiler_params=params(),
    )(z0, z1)


def weight_grad_kernel(x_ref, tg_ref, out_ref):
    total = jnp.zeros(out_ref.shape, f32)
    for r in range(x_ref.shape[0]):
        total += dot(tg_ref[r, :TXT, :192], x_ref[r], 0, 0)
    out_ref[...] = total


def weight_grad(x, tg):
    return pl.pallas_call(
        weight_grad_kernel,
        out_shape=SDS((192, x.shape[2]), f32),
        in_specs=[IN_VMEM] * 2,
        out_specs=IN_VMEM,
        name="weight_grad",
        cost_estimate=cost(4),
        compiler_params=params(),
    )(x, tg)


def local(q_img, k_img, v_img, x_txt, w_txt, grad_img, grad_txt):
    seq, dp = lax.axis_index("seq"), lax.axis_index("dp")
    core = seq % 2
    dp_hi, dp_lo = dp // 4, dp % 4
    pair = [(i, i ^ 1) for i in range(2 * CHIPS)]
    parity = [list(range(j, 2 * CHIPS, 2)) for j in range(2)]
    across = [(i, i ^ 4) for i in range(8)]
    turns = [[(i, i // 4 * 4 + (i + k) % 4) for i in range(8)] for k in range(1, 4)]

    def exchange(x):
        return lax.all_to_all(x, "seq", 0, 0, axis_index_groups=parity, tiled=True)

    def around(x, got):
        both = jnp.stack([x, got])
        return jnp.concatenate([both] + [lax.ppermute(both, "dp", t) for t in turns])

    order = [(dp_hi ^ side) * 4 + (dp_lo + 4 - k) % 4 for k in range(4) for side in range(2)]
    place = [2 * ((dp_lo + 4 - d % 4) % 4) + (dp_hi ^ (d // 4)) for d in range(8)]
    ids = jnp.stack([core] + order + place + [4 * (1 - dp_hi) + 2 * core]).astype(jnp.int32)
    image = (q_img[0], k_img[0], v_img[0], grad_img[0])

    w_own = jnp.swapaxes(w_txt, 1, 2).reshape(192, -1)
    w_across = lax.ppermute(w_own, "dp", across)

    packed = pack(0, *image, 4)
    packed, w_across = lax.optimization_barrier((packed, w_across))
    r0 = exchange(packed)
    weights = around(w_own, w_across)
    text, x8, half = project(ids, x_txt[0], weights, grad_txt[0])
    text_other = lax.ppermute(text, "seq", pair)
    weights_other = lax.ppermute(weights, "seq", pair)
    second = pack(1, *image, 4)
    r0, second, text_other, weights_other, half = lax.optimization_barrier(
        (r0, second, text_other, weights_other, half)
    )

    kv0 = lax.ppermute(r0[:, 1], "seq", pair)
    r1 = exchange(second)
    x_half = lax.ppermute(half, "dp", across)
    y0, ex0, dt0 = attend(0, ids, r0, kv0, text, text_other, 2 * TOK)
    ex0, x_half = lax.optimization_barrier((ex0, x_half))
    got0 = lax.ppermute(ex0, "seq", pair)
    kv1 = lax.ppermute(r1[:, 1], "seq", pair)
    z0 = exchange(finish_first(y0, got0))
    y1, ex1, dt1 = attend(1, ids, r1, kv1, text, text_other, 2 * TOK + DX_ROWS)
    got1 = lax.ppermute(ex1, "seq", pair)

    grads_own, grads_other, o_txt = text_grads(ids, (ex0, got0, dt0, ex1, got1, dt1))
    grads_across = lax.ppermute(grads_own, "dp", across)
    y1 = finish_last(ids, y1, got1, grads_own, grads_other, weights, weights_other)
    y1, grads_across, x_half = lax.optimization_barrier((y1, grads_across, x_half))
    z1 = exchange(y1)
    x_other = lax.ppermute(x_half, "seq", pair)
    x_across = jnp.where(core == 0, jnp.concatenate([x_half, x_other]), jnp.concatenate([x_other, x_half]))
    kept = lax.dynamic_slice_in_dim(x8, 4 * dp_hi, 4, 0)
    both = jnp.stack([kept, x_across], axis=1)
    columns = [lax.dynamic_index_in_dim(both, (dp_lo + k) % 4, 0, keepdims=False) for k in range(4)]
    x_all = jnp.concatenate([columns[0]] + [lax.ppermute(c, "dp", t) for c, t in zip(columns[1:], turns)])
    dw = weight_grad(x_all, around(grads_own, grads_across))
    dw = jnp.swapaxes(dw.reshape(3, 64, -1), 1, 2)
    o_img, grads, dx = unpack(z0, z1, x_txt.shape[2] // (2 * CHIPS))
    return o_img[None], o_txt[None], grads[:, None], dx.transpose(1, 2, 0), dw


def solution(mesh):
    in_specs = (
        P("dp", "seq", None),
        P("dp", "seq", None),
        P("dp", "seq", None),
        P("dp", None, None),
        P(None, "dp", "seq"),
        P("dp", "seq", None),
        P("dp", None, "seq"),
    )
    out_specs = (
        P("dp", "seq", None),
        P("dp", None, "seq"),
        P(None, "dp", "seq", None),
        P("dp", None, "seq"),
        P(None, "dp", "seq"),
    )
    return jax.shard_map(local, mesh=mesh, in_specs=in_specs, out_specs=out_specs, check_vma=False)
```
